256 devices in a mesh: dom: 32 (over y, x, core), sub: 8 (over z).
Axes of the slice: x: 4, y: 4, z: 8, core: 2. Of those that a mesh axis runs over, the one named last changes fastest.
Arguments:
- interior_inverse: bfloat16 [80, 80, 32768], P(None, None, ('dom', 'sub'))
- coupling: bfloat16 [80, 48, 32768], P(None, None, ('dom', 'sub')), may hold values from -0.26953125 to 0.26953125
- trace_block: bfloat16 [48, 48, 32768], P(None, None, ('dom', 'sub'))
- interior_load: bfloat16 [80, 32768], P(None, ('dom', 'sub')), may hold values from -6 to 6
- trace_load: float32 [12, 65536], P(None, ('dom', 'sub'))
- face_shift: float32 [12, 65536], P(None, ('dom', 'sub')), may hold values from 0.2 to 2
- element_faces: int32 [4, 32768], P(None, ('dom', 'sub')), may hold values from 0 to 2175, as said below
- block_padding: int32 [256], P(('dom', 'sub')), may hold values from 0 to 96
Outputs:
- traces: float32 [12, 65536], P(None, ('dom', 'sub'))
- interior: float32 [80, 32768], P(None, ('dom', 'sub'))
The draws below stay inside these ranges and needn't reach their ends.
Inputs may be any that keep to these rules, and one draw needn't show every extreme that they name: `element_faces`: within each partition the indices form one shuffled list: each of the partition's faces except its last 128 is named twice, each of its last 128 faces once, and each index below 128 once.
All inputs are finite; a program needn't handle non-finite values.
Results may differ from the reference program's by a relative error of at most 0.0029.
Values may be sent and summed in bfloat16 or wider, within the bound.
No kernel may reach another device: no remote copies, remote signals or barrier semaphores. Data moves between devices by JAX's collectives and lax.ppermute only.
A program may use at most 64 MiB of HBM per device.

```python
import math
import jax
import jax.numpy as jnp
from jax import lax

NI = 80
FD = 12
NF = 48
BLOCK = 128
RIM = 128
ITERS = 3
ELEM_DEV = 128
ELEM_PART = 1024
FACE_PART = 2048
ELEMS = 32768
FACES = 65536
BLOCKS = 256


def symmetric_blocks(key, order, diagonal_low, diagonal_high, off_bound):
    first, second = jax.random.split(key)
    raw_values = jax.random.uniform(first, (order, order, ELEMS), jnp.float32, -off_bound, off_bound)
    mirrored = 0.5 * (raw_values + jnp.transpose(raw_values, (1, 0, 2)))
    diagonal_values = jax.random.uniform(second, (order, 1, ELEMS), jnp.float32, diagonal_low, diagonal_high)
    row_index = lax.broadcasted_iota(jnp.int32, (order, order, 1), 0)
    column_index = lax.broadcasted_iota(jnp.int32, (order, order, 1), 1)
    return jnp.where(row_index == column_index, diagonal_values, mirrored)


def draw_interior_inverse(key, part):
    return symmetric_blocks(jax.random.fold_in(key, 11), NI, 2.5, 5.0, 2.0 / (NI - 1)).astype(jnp.bfloat16)


def draw_trace_block(key, part):
    return symmetric_blocks(jax.random.fold_in(key, 23), NF, 1.5, 3.0, 1.2 / (NF - 1)).astype(jnp.bfloat16)


def draw_trace_load(key, part):
    first, second = jax.random.split(jax.random.fold_in(key, 37))
    column = jnp.arange(FACES, dtype=jnp.float32)[None, :]
    rising = 1.0 + 2.0 * column / max(FACES - 1, 1)
    scales = jnp.exp(jax.random.uniform(second, (1, FACES), jnp.float32, 0.0, math.log(10.0)))
    base_values = jax.random.normal(first, (FD, FACES), jnp.float32)
    return base_values * scales * rising * 0.25


def draw_element_faces(key, part):
    sequence = jnp.concatenate([RIM + jnp.arange(FACE_PART, dtype=jnp.int32), RIM + jnp.arange(FACE_PART - RIM, dtype=jnp.int32), jnp.arange(RIM, dtype=jnp.int32)])

    def one_partition(number):
        shuffled = jax.random.permutation(jax.random.fold_in(jax.random.fold_in(key, 41), number), 4 * ELEM_PART)
        return sequence[shuffled].reshape(4, ELEM_PART)
    laid_out = jax.vmap(one_partition)(jnp.arange(ELEMS // ELEM_PART, dtype=jnp.int32))
    return jnp.transpose(laid_out, (1, 0, 2)).reshape(4, ELEMS).astype(jnp.int32)


def draw_block_padding(key, part):
    first, second, third = jax.random.split(jax.random.fold_in(key, 53), 3)
    largest = 3 * BLOCK // 4
    values = jax.random.randint(first, (BLOCKS,), 0, largest + 1).astype(jnp.int32)
    top_place = jax.random.randint(second, (), 0, BLOCKS)
    low_place = (top_place + 1 + jax.random.randint(third, (), 0, BLOCKS - 1)) % BLOCKS
    return values.at[top_place].set(largest).at[low_place].set(0)


def block_levels(key, extent, cuts, smallest, high):
    factor_of, own = 1.0, jax.random.fold_in(key, 6)
    for dim, shards_of in cuts:
        heights = jnp.exp(jax.random.uniform(jax.random.fold_in(own, dim), (shards_of,), jnp.float32, smallest / len(cuts), high / len(cuts)))
        factor_of = factor_of * jnp.repeat(heights, extent[dim] // shards_of).reshape([-1 if axis == dim else 1 for axis in range(len(extent))])
    return factor_of


def normal_values(own_key, shape, spread, reach, cuts=(), kind=jnp.bfloat16):
    values = spread * jax.random.normal(own_key, shape, jnp.float32)
    if cuts:
        values = values * block_levels(own_key, shape, cuts, -0.22, 0.18)
    return jnp.clip(values, -reach, reach).astype(kind)


def setup_inputs(seed: int = 0) -> dict:
    keys = jax.random.split(jax.random.key(seed), 9)
    return {
        "interior_inverse": draw_interior_inverse(jax.random.fold_in(keys[8], 71), 0),
        "coupling": normal_values(keys[1], (NI, NF, ELEMS), 0.045, 0.26953125, ((2, 256),)),
        "trace_block": draw_trace_block(jax.random.fold_in(keys[8], 71), 0),
        "interior_load": normal_values(keys[3], (NI, ELEMS), 1.0, 6.0, ((1, 256),)),
        "trace_load": draw_trace_load(jax.random.fold_in(keys[8], 71), 0),
        "face_shift": jnp.clip(jnp.exp(math.log(2.0) - 2.3025851 * jax.random.uniform(keys[5], (FD, FACES), jnp.float32) ** block_levels(keys[5], (FD, FACES), ((1, 256),), -0.2, 0.2)), 0.2, 2.0),
        "element_faces": draw_element_faces(jax.random.fold_in(keys[8], 71), 0),
        "block_padding": draw_block_padding(jax.random.fold_in(keys[8], 71), 0),
    }


precise = lax.Precision.HIGHEST


def halve(value):
    return lax.optimization_barrier(value.astype(jnp.bfloat16)).astype(jnp.float32)


def element_range(interior_inverse, coupling, trace_block, interior_load):
    inverse_wide = interior_inverse.astype(jnp.float32)
    coupling_wide = coupling.astype(jnp.float32)
    coupled = halve(jnp.einsum("ijE,jkE->ikE", inverse_wide, coupling_wide, precision=precise))
    condensed = trace_block.astype(jnp.float32) + jnp.einsum("jiE,jkE->ikE", coupling_wide, coupled, precision=precise)
    solved = jnp.einsum("ijE,jE->iE", inverse_wide, interior_load.astype(jnp.float32), precision=precise)
    pushed = jnp.einsum("jiE,jE->iE", coupling_wide, halve(solved), precision=precise)
    return coupled, condensed, solved, pushed


def face_ids(element_faces):
    column = jnp.arange(ELEMS, dtype=jnp.int32)[None, :]
    partition = column // ELEM_PART
    below_ids = (partition - 1) * FACE_PART + FACE_PART - RIM + element_faces
    below_ids = jnp.where(partition > 0, below_ids, FACES)
    own_ids = partition * FACE_PART + element_faces - RIM
    return jnp.where(element_faces < RIM, below_ids, own_ids).astype(jnp.int32).reshape(-1)


def reference(interior_inverse, coupling, trace_block, interior_load, trace_load, face_shift, element_faces, block_padding):
    position = jnp.arange(ELEMS, dtype=jnp.int32)
    padding_here = jnp.repeat(block_padding, BLOCK, total_repeat_length=ELEMS)
    living = ((position % BLOCK) < BLOCK - padding_here).astype(jnp.float32)
    identity_ids = face_ids(element_faces)

    def view(vector):
        padded = jnp.concatenate([vector, jnp.zeros((FD, 1), jnp.float32)], axis=1)
        return padded[:, identity_ids].reshape(NF, ELEMS)

    def assemble(element_terms):
        summed = jnp.zeros((FD, FACES + 1), jnp.float32).at[:, identity_ids].add(element_terms.reshape(FD, -1))
        return summed[:, :FACES]

    def portion_slice(array, start):
        return lax.dynamic_slice_in_dim(array, start, ELEM_DEV, array.ndim - 1)

    def first_pass(counter, state_now):
        condensed_all, solved_all, pushed_all = state_now
        start = jnp.asarray(counter).astype(jnp.int32) * ELEM_DEV
        unused, condensed, solved, pushed = element_range(portion_slice(interior_inverse, start), portion_slice(coupling, start), portion_slice(trace_block, start), portion_slice(interior_load, start))
        condensed_all = lax.dynamic_update_slice_in_dim(condensed_all, condensed, start, 2)
        solved_all = lax.dynamic_update_slice_in_dim(solved_all, solved, start, 1)
        pushed_all = lax.dynamic_update_slice_in_dim(pushed_all, pushed, start, 1)
        return condensed_all, solved_all, pushed_all

    initial = (jnp.zeros((NF, NF, ELEMS), jnp.float32), jnp.zeros((NI, ELEMS), jnp.float32), jnp.zeros((NF, ELEMS), jnp.float32))
    condensed_all, solved_all, pushed_all = lax.fori_loop(0, ELEMS // ELEM_DEV, first_pass, initial)

    right_side = trace_load + assemble(pushed_all * living)

    def operate(vector):
        element_terms = jnp.einsum("ijE,jE->iE", condensed_all, view(vector), precision=precise) * living
        return assemble(element_terms) + face_shift * vector

    traces = jnp.zeros_like(right_side)
    residual = right_side
    direction = right_side
    norm_now = jnp.sum(residual * residual)
    for iteration in range(ITERS):
        image = operate(direction)
        step_size = norm_now / jnp.sum(direction * image)
        traces = traces + step_size * direction
        residual = residual - step_size * image
        norm_next = jnp.sum(residual * residual)
        direction = residual + (norm_next / norm_now) * direction
        norm_now = norm_next

    traces_half = halve(view(traces))

    def second_pass(counter, interior_all):
        start = jnp.asarray(counter).astype(jnp.int32) * ELEM_DEV
        coupled, unused_a, unused_b, unused_c = element_range(portion_slice(interior_inverse, start), portion_slice(coupling, start), portion_slice(trace_block, start), portion_slice(interior_load, start))
        lifted = jnp.einsum("ijE,jE->iE", coupled, portion_slice(traces_half, start), precision=precise)
        result = (portion_slice(solved_all, start) - lifted) * portion_slice(living, start)
        return lax.dynamic_update_slice_in_dim(interior_all, result, start, 1)

    interior = lax.fori_loop(0, ELEMS // ELEM_DEV, second_pass, jnp.zeros((NI, ELEMS), jnp.float32))
    return traces, interior
```

```python
import functools

import jax
import jax.numpy as jnp
from jax import lax
from jax.experimental import pallas as pl
from jax.experimental.pallas import tpu as pltpu
from jax.sharding import PartitionSpec as P

NI = 80
FD = 12
NF = 48
LANES = 128
RIM = 128
SUB = 8
FACES_PART = 2048
F32 = jnp.float32
BF16 = jnp.bfloat16
VMEM_LIMIT = 24 * 1024 * 1024

PUSHED, UP, DOWN, LOADS, SHIFTS, NAMES, FIRST_ROWS = 0, 48, 72, 84, 108, 132, 136
LATER_UP, LATER_DOWN, LATER_ROWS = 48, 60, 72


def row_iota(rows):
    return lax.broadcasted_iota(jnp.int32, (rows, LANES), 0)


def lane_iota(rows):
    return lax.broadcasted_iota(jnp.int32, (rows, LANES), 1)


def eight_sums(parts):
    rows = row_iota(8)
    low = rows < 4
    parts = [
        jnp.where(low, parts[i], parts[i + 4])
        + pltpu.roll(jnp.where(low, parts[i + 4], parts[i]), 4, 0)
        for i in range(4)
    ]
    for step in (2, 1):
        low = (rows & step) == 0
        parts = [
            jnp.where(
                low,
                parts[i] + pltpu.roll(parts[i], 8 - step, 0),
                parts[i + step] + pltpu.roll(parts[i + step], step, 0),
            )
            for i in range(step)
        ]
    return parts[0]


def matrix_times(matrix_ref, vector):
    rows, depth, _ = matrix_ref.shape
    blocks = []
    for first in range(0, rows, 8):
        parts = [
            (matrix_ref[first + i].astype(F32) * vector)
            .reshape(depth // 8, 8, LANES)
            .sum(0)
            for i in range(8)
        ]
        blocks.append(eight_sums(parts))
    return jnp.concatenate(blocks, 0)


def transposed_times(matrix_ref, vector):
    depth = matrix_ref.shape[0]
    totals = [None, None]
    for i in range(depth):
        term = matrix_ref[i].astype(F32) * vector[i : i + 1]
        totals[i % 2] = term if totals[i % 2] is None else totals[i % 2] + term
    return totals[0] + totals[1]


def living_mask(padding_ref):
    return lane_iota(1) < LANES - padding_ref[0]


def element_operator(inverse_ref, coupling_ref, trace_ref, view, living):
    inner = matrix_times(inverse_ref, matrix_times(coupling_ref, view))
    terms = transposed_times(coupling_ref, inner) + matrix_times(trace_ref, view)
    return jnp.where(living, terms, 0.0)


def split3(value):
    high = value.astype(BF16)
    rest = value - high.astype(F32)
    middle = rest.astype(BF16)
    low = (rest - middle.astype(F32)).astype(BF16)
    return high, middle, low


def exact_pick(values, chosen):
    stacked = jnp.concatenate(split3(values), 0)
    sums = lax.dot_general(
        stacked, chosen, (((1,), (1,)), ((), ())), preferred_element_type=F32
    )
    rows = values.shape[0]
    return sums[:rows] + sums[rows : 2 * rows] + sums[2 * rows :]


def face_major(terms_ref):
    slots = []
    for j in range(4):
        part = terms_ref[pl.ds(j, FD, stride=4), :]
        slots.append(jnp.concatenate([part, jnp.zeros((4, LANES), F32)], 0))
    return jnp.concatenate(slots, 1)


def rim_lists(terms_ref, names_ref):
    wanted = lax.broadcasted_iota(jnp.int32, (2 * RIM, LANES), 0)
    wanted = jnp.where(wanted < RIM, wanted, wanted + FACES_PART - RIM)
    chosen = [
        jnp.where(wanted == names_ref[j : j + 1, :], 1.0, 0.0).astype(BF16)
        for j in range(4)
    ]
    lists = exact_pick(face_major(terms_ref), jnp.concatenate(chosen, 1))
    return lists[:FD, :RIM], lists[:FD, RIM:]


def first_kernel(
    ids_ref, padding_ref, inverse_ref, coupling_ref, interior_load_ref, trace_load_ref, shift_ref, names_ref,
    solved_ref, pushed_ref, up_ref, down_ref,
):
    living = living_mask(padding_ref)
    solved = matrix_times(inverse_ref, interior_load_ref[...].astype(F32))
    solved_ref[...] = solved
    pushed_ref[...] = jnp.where(living, transposed_times(coupling_ref, solved), 0.0)
    low, high = rim_lists(pushed_ref, names_ref)
    owner = ids_ref[1] == SUB - 1
    up_ref[:FD, :] = high + jnp.where(owner, trace_load_ref[:, RIM:], 0.0)
    up_ref[FD:, :] = jnp.where(owner, shift_ref[:, RIM:], 0.0)
    down_ref[...] = low


def spread_rows(values, block):
    a = jnp.broadcast_to(values[2 * block : 2 * block + 1], (8, LANES))
    b = jnp.broadcast_to(values[2 * block + 1 : 2 * block + 2], (8, LANES))
    return jnp.where(row_iota(8) < 4, a, b)


def turn(values, steps):
    if steps == 0:
        return values
    rows = row_iota(8) & 3
    return jnp.where(
        rows < 4 - steps, pltpu.roll(values, 8 - steps, 0), pltpu.roll(values, 4 - steps, 0)
    )


def take_lanes(values, lanes):
    return jnp.take_along_axis(values, lanes, axis=1, mode="promise_in_bounds")


def partner_terms(gathered_ref, chunk, lane, low_list, high_list):
    rows = row_iota(8) & 3
    found = [jnp.zeros((8, LANES), F32) for _ in range(6)]
    for t in range(4):
        chunk_t = turn(chunk, (4 - t) % 4)
        lane_t = turn(lane, (4 - t) % 4)
        part = [jnp.zeros((8, LANES), F32) for _ in range(6)]
        for s in range(SUB):
            here = chunk_t == 4 * s + rows
            for g in range(6):
                taken = take_lanes(gathered_ref[s, 8 * g : 8 * g + 8, :], lane_t)
                part[g] = jnp.where(here, taken, part[g])
        for g in range(6):
            found[g] = found[g] + turn(part[g], t)
    on_low = chunk == 4 * SUB
    on_high = chunk == 4 * SUB + 1
    for g in range(6):
        found[g] = jnp.where(on_low, take_lanes(spread_rows(low_list, g), lane), found[g])
        found[g] = jnp.where(on_high, take_lanes(spread_rows(high_list, g), lane), found[g])
    return jnp.concatenate(found, 0)


def twice(slots):
    return jnp.concatenate([slots, slots], 0)


def six_times(rows8):
    return jnp.concatenate([rows8] * 6, 0)


def summed(gathered_ref, first, last):
    total = gathered_ref[0, first:last, :]
    for s in range(1, SUB):
        total = total + gathered_ref[s, first:last, :]
    return total


def partner_places(names_ref, gathered_ref, sub):
    weights, columns = [], []
    high_rows = row_iota(24)
    low_rows = row_iota(LANES)
    for s in range(SUB):
        for j in range(4):
            names = gathered_ref[s, NAMES + j : NAMES + j + 1, :].astype(jnp.int32)
            row_hit = (names >> 7) == high_rows
            weights.append(
                jnp.concatenate(
                    [
                        jnp.where(row_hit, F32(4 * s + j), 0.0),
                        jnp.where(row_hit, lane_iota(24).astype(F32), 0.0),
                    ],
                    0,
                ).astype(BF16)
            )
            columns.append(jnp.where((names & 127) == low_rows, 1.0, 0.0).astype(BF16))
    table = lax.dot_general(
        jnp.concatenate(weights, 1),
        jnp.concatenate(columns, 1),
        (((1,), (1,)), ((), ())),
        preferred_element_type=F32,
    )
    chunks, lanes = [], []
    for j in range(4):
        name = names_ref[j : j + 1, :]
        low = jnp.broadcast_to(name & 127, (24, LANES))
        hit = high_rows == (name >> 7)
        chunk_sum = jnp.where(hit, take_lanes(table[:24], low), 0.0).sum(0, keepdims=True)
        lane_sum = jnp.where(hit, take_lanes(table[24:], low), 0.0).sum(0, keepdims=True)
        chunk = chunk_sum.astype(jnp.int32) - (4 * sub + j)
        lane = lane_sum.astype(jnp.int32) - lane_iota(1)
        below, above = name < RIM, name >= FACES_PART
        chunk = jnp.where(below, 4 * SUB, jnp.where(above, 4 * SUB + 1, chunk))
        lane = jnp.where(below | above, name & 127, lane)
        chunks.append(chunk)
        lanes.append(lane)
    return jnp.concatenate(chunks, 0), jnp.concatenate(lanes, 0) & 127


def face_values(names_ref, gathered_ref, up_list, loads_ref, shifts_ref):
    for j in range(4):
        name = names_ref[j : j + 1, :]
        high = jnp.broadcast_to(name >> 7, (24, LANES))
        low = jnp.broadcast_to(name & 127, (24, LANES))
        got = jnp.where(high == 0, take_lanes(up_list, low), 0.0)
        for s in range(SUB):
            for half in range(2):
                source = jnp.concatenate(
                    [
                        gathered_ref[s, LOADS + 12 * half : LOADS + 12 * half + 12, :],
                        gathered_ref[s, SHIFTS + 12 * half : SHIFTS + 12 * half + 12, :],
                    ],
                    0,
                )
                got = jnp.where(high == 2 * s + half + 1, take_lanes(source, low), got)
        loads_ref[pl.ds(j, FD, stride=4), :] = got[:FD]
        shifts_ref[pl.ds(j, FD, stride=4), :] = got[FD:]


def second_kernel(
    ids_ref, padding_ref, inverse_ref, coupling_ref, trace_ref, names_ref, pushed_ref, gathered_ref,
    chunk_ref, lane_ref, valid_ref, weight_ref, shifts_ref, view_ref, terms_ref, up_ref, down_ref,
    loads_ref,
):
    dom, sub = ids_ref[0], ids_ref[1]
    chunk, lane = partner_places(names_ref, gathered_ref, sub)
    chunk, lane = twice(chunk), twice(lane)
    names = twice(names_ref[...])
    valid = jnp.where((names < RIM) & (dom == 0), 0.0, 1.0)
    weight = jnp.where((names >= FACES_PART) & (dom == ids_ref[2] - 1), 1.0, 0.5)
    chunk_ref[...] = chunk
    lane_ref[...] = lane
    valid_ref[...] = valid
    weight_ref[...] = weight
    up_list = summed(gathered_ref, UP, UP + 24)
    down_list = summed(gathered_ref, DOWN, DOWN + 12)
    face_values(names_ref, gathered_ref, up_list, loads_ref, shifts_ref)
    own_load = jnp.where(six_times(names) < RIM, 0.0, loads_ref[...])
    partner = partner_terms(gathered_ref, chunk, lane, up_list[:FD], down_list)
    view = jnp.where(six_times(valid) > 0.0, own_load + (pushed_ref[...] + partner), 0.0)
    view_ref[...] = view
    terms_ref[...] = element_operator(
        inverse_ref, coupling_ref, trace_ref, view, living_mask(padding_ref)
    )
    low, high = rim_lists(terms_ref, names_ref)
    up_ref[...] = high
    down_ref[...] = low


def next_view(gathered_ref, chunk_ref, lane_ref, valid_ref, shifts_ref, view_ref, terms_ref):
    low_list = summed(gathered_ref, LATER_UP, LATER_UP + FD)
    high_list = summed(gathered_ref, LATER_DOWN, LATER_DOWN + FD)
    partner = partner_terms(gathered_ref, chunk_ref[...], lane_ref[...], low_list, high_list)
    image = terms_ref[...] + partner + shifts_ref[...] * view_ref[...]
    return jnp.where(six_times(valid_ref[...]) > 0.0, image, 0.0)


def third_kernel(
    padding_ref, inverse_ref, coupling_ref, trace_ref, names_ref, gathered_ref,
    chunk_ref, lane_ref, valid_ref, shifts_ref, view_ref, terms_ref,
    new_view_ref, new_terms_ref, up_ref, down_ref,
):
    view = next_view(gathered_ref, chunk_ref, lane_ref, valid_ref, shifts_ref, view_ref, terms_ref)
    new_view_ref[...] = view
    new_terms_ref[...] = element_operator(
        inverse_ref, coupling_ref, trace_ref, view, living_mask(padding_ref)
    )
    low, high = rim_lists(new_terms_ref, names_ref)
    up_ref[...] = high
    down_ref[...] = low


def fourth_kernel(
    padding_ref, inverse_ref, coupling_ref, trace_ref, gathered_ref,
    chunk_ref, lane_ref, valid_ref, weight_ref, shifts_ref, first_view_ref, view_ref, terms_ref,
    new_view_ref, sums_ref,
):
    first, second = first_view_ref[...], view_ref[...]
    third = next_view(gathered_ref, chunk_ref, lane_ref, valid_ref, shifts_ref, view_ref, terms_ref)
    new_view_ref[...] = third
    last = element_operator(inverse_ref, coupling_ref, trace_ref, third, living_mask(padding_ref))
    weight = six_times(weight_ref[...])
    last = last + weight * (shifts_ref[...] * third)
    views = (first, second, third)
    products = [weight * views[i] * views[j] for i in range(3) for j in range(i, 3)]
    products += [view * last for view in views]
    lane = lane_iota(1)
    sums = jnp.zeros((1, LANES), F32)
    for place, product in enumerate(products):
        total = product.reshape(6, 8, LANES).sum(0).sum(0, keepdims=True).sum(1, keepdims=True)
        sums = sums + jnp.where(lane == place, total, 0.0)
    sums_ref[...] = sums


def owner_kernel(
    ids_ref, first_ref, second_ref, third_ref, trace_load_ref, shift_ref,
    owned_ref, terms_ref, chosen_ref,
):
    sub = ids_ref[1]
    wanted = lax.broadcasted_iota(jnp.int32, (2 * RIM, LANES), 0) + (RIM + 2 * RIM * sub)
    sources = (first_ref, second_ref, third_ref)
    for s in range(SUB):
        for j in range(4):
            columns = slice((4 * s + j) * LANES, (4 * s + j + 1) * LANES)
            names = first_ref[s, NAMES + j : NAMES + j + 1, :].astype(jnp.int32)
            chosen_ref[:, columns] = jnp.where(wanted == names, 1.0, 0.0).astype(BF16)
            for v, source in enumerate(sources):
                part = source[s, pl.ds(j, FD, stride=4), :]
                part = jnp.concatenate([part, jnp.zeros((4, LANES), F32)], 0)
                for piece, value in enumerate(split3(part)):
                    first = 16 * (3 * v + piece)
                    terms_ref[first : first + 16, columns] = value
    sums = lax.dot_general(
        terms_ref[...], chosen_ref[...], (((1,), (1,)), ((), ())), preferred_element_type=F32
    )
    last = sub == SUB - 1
    downs = (
        summed(first_ref, DOWN, DOWN + FD),
        summed(second_ref, LATER_DOWN, LATER_DOWN + FD),
        summed(third_ref, LATER_DOWN, LATER_DOWN + FD),
    )
    current = None
    for v in range(3):
        rows = [sums[48 * v + 16 * piece : 48 * v + 16 * piece + FD] for piece in range(3)]
        total = rows[0] + rows[1] + rows[2]
        down = jnp.concatenate(
            [jnp.zeros((FD, RIM), F32), jnp.where(last, downs[v], 0.0)], 1
        )
        total = total + down
        if v == 0:
            current = total + trace_load_ref[...]
        else:
            current = total + shift_ref[...] * current
        owned_ref[v] = current


def coefficients(sums):
    lane = lane_iota(1)

    def entry(place):
        return jnp.where(lane == place, sums, 0.0).sum(1, keepdims=True)

    table = {}
    place = 0
    for i in range(3):
        for j in range(i, 3):
            table[i, j] = table[j, i] = entry(place)
            place += 1
    for i in range(3):
        table[i, 3] = entry(place)
        place += 1

    def form(left, right):
        total = None
        for i, a in enumerate(left):
            for j, b in enumerate(right):
                if a is None or b is None:
                    continue
                term = a * b * table[i, j]
                total = term if total is None else total + term
        return total

    def combine(left, factor, right):
        merged = []
        for i in range(max(len(left), len(right))):
            a = left[i] if i < len(left) else None
            b = right[i] if i < len(right) else None
            if b is None:
                merged.append(a)
            else:
                merged.append(factor * b if a is None else a + factor * b)
        return merged

    one = jnp.ones((1, 1), F32)
    residual, direction, result = [one], [one], []
    norm = table[0, 0]
    for iteration in range(3):
        image = [None] + direction
        step = norm / form(direction, image)
        result = combine(result, step, direction)
        if iteration < 2:
            residual = combine(residual, -step, image)
            new_norm = form(residual, residual)
            direction = combine(residual, new_norm / norm, direction)
            norm = new_norm
    return result


def last_kernel(
    padding_ref, inverse_ref, coupling_ref, all_sums_ref, first_view_ref, second_view_ref, third_view_ref,
    solved_ref, owned_ref,
    traces_ref, interior_ref,
):
    sums = all_sums_ref[...].reshape(-1, 8, LANES).sum(0).sum(0, keepdims=True)
    a, b, c = coefficients(sums)
    traces_ref[...] = a * owned_ref[0] + b * owned_ref[1] + c * owned_ref[2]
    view = a * first_view_ref[...] + b * second_view_ref[...] + c * third_view_ref[...]
    lifted = matrix_times(inverse_ref, matrix_times(coupling_ref, view))
    interior_ref[...] = jnp.where(living_mask(padding_ref), solved_ref[...] - lifted, 0.0)


def call(kernel, outputs, inputs, scalars=0, scratch=()):
    shape = [jax.ShapeDtypeStruct(s, d) for s, d in outputs]
    return pl.pallas_call(
        kernel,
        out_shape=shape,
        in_specs=[
            pl.BlockSpec(memory_space=pltpu.SMEM if i < scalars else pltpu.VMEM)
            for i in range(len(inputs))
        ],
        out_specs=[pl.BlockSpec(memory_space=pltpu.VMEM)] * len(shape),
        scratch_shapes=list(scratch),
        compiler_params=pltpu.CompilerParams(vmem_limit_bytes=VMEM_LIMIT),
    )(*inputs)


def to_all(value):
    copies = jnp.broadcast_to(value[None], (SUB,) + value.shape)
    return lax.all_to_all(copies, "sub", 0, 0, tiled=True)


def neighbours(up, down):
    count = lax.axis_size("dom")
    from_below = lax.ppermute(up, "dom", [(i, i + 1) for i in range(count - 1)])
    from_above = lax.ppermute(down, "dom", [(i + 1, i) for i in range(count - 1)])
    return from_below, from_above


def on_device(
    interior_inverse, coupling, trace_block, interior_load, trace_load, face_shift, element_faces, block_padding,
):
    ids = jnp.stack(
        [lax.axis_index("dom"), lax.axis_index("sub"), jnp.int32(lax.axis_size("dom"))]
    ).astype(jnp.int32)
    slab, lists = ((NF, LANES), F32), ((FD, LANES), F32)
    solved, pushed, up, down = call(
        first_kernel,
        [((NI, LANES), F32), slab, ((2 * FD, LANES), F32), lists],
        [ids, block_padding, interior_inverse, coupling, interior_load, trace_load, face_shift, element_faces],
        scalars=2,
    )
    from_below, from_above = neighbours(up, down)
    first = to_all(
        jnp.concatenate(
            [
                pushed, from_below, from_above,
                trace_load[:, :RIM], trace_load[:, RIM:], face_shift[:, :RIM], face_shift[:, RIM:],
                element_faces.astype(F32),
            ],
            0,
        )
    )
    eight_i, eight_f = ((8, LANES), jnp.int32), ((8, LANES), F32)
    chunk, lane, valid, weight, shifts, view0, terms, up, down = call(
        second_kernel,
        [eight_i, eight_i, eight_f, eight_f, slab, slab, slab, lists, lists],
        [ids, block_padding, interior_inverse, coupling, trace_block, element_faces, pushed, first],
        scalars=2,
        scratch=[pltpu.VMEM((NF, LANES), F32)],
    )
    second = to_all(jnp.concatenate([terms, *neighbours(up, down)], 0))
    view1, terms1, up, down = call(
        third_kernel,
        [slab, slab, lists, lists],
        [block_padding, interior_inverse, coupling, trace_block, element_faces, second, chunk, lane, valid, shifts, view0, terms],
        scalars=1,
    )
    third = to_all(jnp.concatenate([terms1, *neighbours(up, down)], 0))
    view2, sums = call(
        fourth_kernel,
        [slab, ((1, LANES), F32)],
        [block_padding, interior_inverse, coupling, trace_block, third, chunk, lane, valid, weight, shifts, view0, view1, terms1],
        scalars=1,
    )
    everyone = lax.axis_size("dom") * SUB
    all_sums = lax.all_to_all(
        jnp.broadcast_to(sums, (everyone, LANES)), ("dom", "sub"), 0, 0, tiled=True
    )
    (owned,) = call(
        owner_kernel,
        [((3, FD, 2 * RIM), F32)],
        [ids, first, second, third, trace_load, face_shift],
        scalars=1,
        scratch=[pltpu.VMEM((144, 32 * LANES), BF16), pltpu.VMEM((2 * RIM, 32 * LANES), BF16)],
    )
    traces, interior = call(
        last_kernel,
        [((FD, 2 * RIM), F32), ((NI, LANES), F32)],
        [block_padding, interior_inverse, coupling, all_sums, view0, view1, view2, solved, owned],
        scalars=1,
    )
    return traces, interior


def solution(mesh):
    last = ("dom", "sub")
    placed = (
        P(None, None, last), P(None, None, last), P(None, None, last),
        P(None, last), P(None, last), P(None, last), P(None, last), P(last),
    )
    return jax.shard_map(
        on_device,
        mesh=mesh,
        in_specs=placed,
        out_specs=(P(None, last), P(None, last)),
        check_vma=False,
    )
```

```python
import functools

import jax
import jax.numpy as jnp
from jax import lax
from jax.experimental import pallas as pl
from jax.experimental.pallas import tpu as pltpu
from jax.sharding import PartitionSpec as P

NI = 80
FD = 12
NF = 48
LANES = 128
RIM = 128
SUB = 8
FACES_PART = 2048
F32 = jnp.float32
BF16 = jnp.bfloat16
MIB = 1024 * 1024
PARTS = 5

I16 = jnp.int16

PUSHED, LOADS, SHIFTS, NAMES, SCALES, UP, UP_SHIFT, DOWN, FIRST_END, FIRST_ROWS = (
    0, 48, 72, 96, 100, 103, 116, 129, 142, 144,
)
LATER_UP, LATER_DOWN, LATER_END, LATER_ROWS = 49, 62, 75, 80


def row_iota(rows):
    return lax.broadcasted_iota(jnp.int32, (rows, LANES), 0)


def lane_iota(rows):
    return lax.broadcasted_iota(jnp.int32, (rows, LANES), 1)


def eight_sums(parts):
    rows = row_iota(8)
    low = rows < 4
    parts = [
        jnp.where(low, parts[i], parts[i + 4])
        + pltpu.roll(jnp.where(low, parts[i + 4], parts[i]), 4, 0)
        for i in range(4)
    ]
    for step in (2, 1):
        low = (rows & step) == 0
        parts = [
            jnp.where(
                low,
                parts[i] + pltpu.roll(parts[i], 8 - step, 0),
                parts[i + step] + pltpu.roll(parts[i + step], step, 0),
            )
            for i in range(step)
        ]
    return parts[0]


def matrix_times(matrix_ref, vector):
    rows, depth, _ = matrix_ref.shape
    blocks = []
    for first in range(0, rows, 8):
        parts = [
            (matrix_ref[first + i].astype(F32) * vector)
            .reshape(depth // 8, 8, LANES)
            .sum(0)
            for i in range(8)
        ]
        blocks.append(eight_sums(parts))
    return jnp.concatenate(blocks, 0)


def transposed_times(matrix_ref, vector):
    depth = matrix_ref.shape[0]
    totals = [None, None]
    for i in range(depth):
        term = matrix_ref[i].astype(F32) * vector[i : i + 1]
        totals[i % 2] = term if totals[i % 2] is None else totals[i % 2] + term
    return totals[0] + totals[1]


def coded(value):
    top = jnp.abs(value).max(0, keepdims=True).max(1, keepdims=True)
    exponent = jnp.floor(jnp.log2(jnp.maximum(top, 2.0**-100))) + 1.0
    whole = jnp.floor(value * jnp.exp2(15.0 - exponent) + 0.5)
    return jnp.clip(whole, -32767.0, 32767.0), exponent


def spread_row(exponent):
    return jnp.broadcast_to(exponent, (1, LANES))


def as_sent(value):
    return value.astype(jnp.int32).astype(I16)


def with_exponent(value):
    whole, exponent = coded(value)
    return [whole, spread_row(exponent)]


def put_lists(on_ref, off_ref, up, down, dom):
    even = dom % 2 == 0
    rest = [jnp.zeros((on_ref.shape[0] - sum(len(x) for x in up), LANES), F32)]
    up, down = jnp.concatenate(up + rest, 0), jnp.concatenate(down + rest, 0)
    on_ref[...] = as_sent(jnp.where(even, up, down))
    off_ref[...] = as_sent(jnp.where(even, down, up))


def decode(sent_ref, terms_ref, sections):
    rows = sent_ref.shape[1]
    row = row_iota(rows)
    for s in range(SUB):
        values = sent_ref[s].astype(jnp.int32).astype(F32)
        terms_ref[s] = values
        factors = jnp.ones((1, LANES), F32)
        for end, exponent in reversed(sections):
            if exponent is None:
                factor = jnp.ones((1, LANES), F32)
            else:
                factor = jnp.exp2(terms_ref[s, exponent : exponent + 1, :] - 15.0)
            factors = jnp.where(row < end, factor, factors)
        terms_ref[s] = values * factors


def decode_first(sent_ref, terms_ref):
    decode(
        sent_ref,
        terms_ref,
        [
            (LOADS, SCALES), (SHIFTS, SCALES + 1), (NAMES, SCALES + 2), (UP, None),
            (UP + FD, UP + FD), (UP_SHIFT, None), (UP_SHIFT + FD, UP_SHIFT + FD), (DOWN, None),
            (FIRST_END, DOWN + FD),
        ],
    )


def decode_later(sent_ref, terms_ref):
    decode(
        sent_ref,
        terms_ref,
        [(NF, NF), (LATER_UP, None), (LATER_UP + FD, LATER_UP + FD), (LATER_DOWN, None), (LATER_END, LATER_DOWN + FD)],
    )


def ids():
    return lax.axis_index("dom"), lax.axis_index("sub")


def element_operator(inverse_ref, coupling_ref, trace_ref, view, living_ref, keep):
    inner = matrix_times(inverse_ref, matrix_times(coupling_ref, view))
    keep(inner)
    terms = transposed_times(coupling_ref, inner) + matrix_times(trace_ref, view)
    return jnp.where(six_times(living_ref[...]) > 0.0, terms, 0.0)


def split3(value):
    high = value.astype(BF16)
    rest = value - high.astype(F32)
    middle = rest.astype(BF16)
    low = (rest - middle.astype(F32)).astype(BF16)
    return high, middle, low


def whole_pick(values, chosen):
    high = jnp.floor(values * (1.0 / 256.0))
    stacked = jnp.concatenate([high, values - 256.0 * high], 0).astype(BF16)
    sums = lax.dot_general(
        stacked, chosen, (((1,), (1,)), ((), ())), preferred_element_type=F32
    )
    rows = values.shape[0]
    return 256.0 * sums[:rows] + sums[rows:]


def face_major(terms_ref):
    slots = []
    for j in range(4):
        part = terms_ref[pl.ds(j, FD, stride=4), :]
        slots.append(jnp.concatenate([part, jnp.zeros((4, LANES), F32)], 0))
    return jnp.concatenate(slots, 1)


def rim_lists(terms_ref, names_ref):
    wanted = lax.broadcasted_iota(jnp.int32, (2 * RIM, LANES), 0)
    wanted = jnp.where(wanted < RIM, wanted, wanted + FACES_PART - RIM)
    chosen = [
        jnp.where(wanted == names_ref[j : j + 1, :], 1.0, 0.0).astype(BF16)
        for j in range(4)
    ]
    lists = whole_pick(face_major(terms_ref), jnp.concatenate(chosen, 1))
    return lists[:FD, :RIM], lists[:FD, RIM:]


def first_kernel(
    inverse_hbm, coupling_hbm, interior_load_hbm, trace_load_hbm, shift_hbm, names_hbm, padding_hbm,
    living_ref, own_ref, on_ref, off_ref, solved_hbm,
    solved_ref, inverse_ref, coupling_ref, interior_load_ref, trace_load_ref, shift_ref, names_ref, padding_ref, stage_ref, sems,
):
    rows = NI // PARTS
    copies = [pltpu.make_async_copy(interior_load_hbm, interior_load_ref, sems.at[0])]
    for part in range(PARTS):
        block = pl.ds(part * rows, rows)
        copies.append(
            pltpu.make_async_copy(inverse_hbm.at[block], inverse_ref.at[block], sems.at[1 + part])
        )
    rest = [
        (coupling_hbm, coupling_ref), (names_hbm, names_ref),
        (trace_load_hbm, trace_load_ref), (shift_hbm, shift_ref), (padding_hbm, padding_ref),
    ]
    for place, (source, target) in enumerate(rest):
        copies.append(pltpu.make_async_copy(source, target, sems.at[1 + PARTS + place]))
    for copy in copies:
        copy.start()
    dom, sub = ids()
    for copy in copies[2 + PARTS :]:
        copy.wait()
    padding = jnp.broadcast_to(padding_ref[:, :1], (1, LANES))
    living = lane_iota(1) < LANES - padding
    living_ref[...] = jnp.broadcast_to(jnp.where(living, 1.0, 0.0), (8, LANES))
    stage_ref[NAMES:, :] = jnp.zeros((stage_ref.shape[0] - NAMES, LANES), F32)
    loads, load_exponent = coded(trace_load_ref[...])
    shifts, shift_exponent = coded(shift_ref[...])
    for half in range(2):
        columns = slice(half * RIM, half * RIM + RIM)
        stage_ref[LOADS + FD * half : LOADS + FD * half + FD, :] = loads[:, columns]
        stage_ref[SHIFTS + FD * half : SHIFTS + FD * half + FD, :] = shifts[:, columns]
    stage_ref[NAMES : NAMES + 4, :] = names_ref[...].astype(F32)
    stage_ref[SCALES + 1 : SCALES + 2, :] = spread_row(load_exponent)
    stage_ref[SCALES + 2 : SCALES + 3, :] = spread_row(shift_exponent)
    copies[0].wait()
    load = interior_load_ref[...].astype(F32)
    solved = []
    for part in range(PARTS):
        copies[1 + part].wait()
        solved.append(matrix_times(inverse_ref.at[pl.ds(part * rows, rows)], load))
    solved = jnp.concatenate(solved, 0)
    solved_ref[...] = solved
    keep = pltpu.make_async_copy(solved_ref, solved_hbm, sems.at[PARTS + 6])
    keep.start()
    copies[1 + PARTS].wait()
    whole, exponent = coded(jnp.where(living, transposed_times(coupling_ref, solved), 0.0))
    stage_ref[:NF, :] = whole
    stage_ref[SCALES : SCALES + 1, :] = spread_row(exponent)
    low, high = rim_lists(stage_ref, names_ref)
    owner = sub == SUB - 1
    up = with_exponent(
        high * jnp.exp2(exponent - 15.0) + jnp.where(owner, trace_load_ref[:, RIM:], 0.0)
    )
    up += [jnp.where(owner, shifts[:, RIM:], 0.0), spread_row(shift_exponent)]
    down = [low, spread_row(exponent), jnp.zeros((FD + 1, LANES), F32)]
    put_lists(on_ref, off_ref, up, down, dom)
    own_ref[...] = as_sent(stage_ref[...])
    keep.wait()


def spread_rows(values, block):
    a = jnp.broadcast_to(values[2 * block : 2 * block + 1], (8, LANES))
    b = jnp.broadcast_to(values[2 * block + 1 : 2 * block + 2], (8, LANES))
    return jnp.where(row_iota(8) < 4, a, b)


def turn(values, steps):
    if steps == 0:
        return values
    rows = row_iota(8) & 3
    return jnp.where(
        rows < 4 - steps, pltpu.roll(values, 8 - steps, 0), pltpu.roll(values, 4 - steps, 0)
    )


def take_lanes(values, lanes):
    return jnp.take_along_axis(values, lanes, axis=1, mode="promise_in_bounds")


def partner_terms(gathered_ref, chunk, lane, low_list, high_list):
    rows = row_iota(8) & 3
    found = [jnp.zeros((8, LANES), F32) for _ in range(6)]
    for t in range(4):
        chunk_t = turn(chunk, (4 - t) % 4)
        lane_t = turn(lane, (4 - t) % 4)
        part = [jnp.zeros((8, LANES), F32) for _ in range(6)]
        for s in range(SUB):
            here = chunk_t == 4 * s + rows
            for g in range(6):
                taken = take_lanes(gathered_ref[s, 8 * g : 8 * g + 8, :], lane_t)
                part[g] = jnp.where(here, taken, part[g])
        for g in range(6):
            found[g] = found[g] + turn(part[g], t)
    on_low = chunk == 4 * SUB
    on_high = chunk == 4 * SUB + 1
    for g in range(6):
        found[g] = jnp.where(on_low, take_lanes(spread_rows(low_list, g), lane), found[g])
        found[g] = jnp.where(on_high, take_lanes(spread_rows(high_list, g), lane), found[g])
    return jnp.concatenate(found, 0)


def twice(slots):
    return jnp.concatenate([slots, slots], 0)


def six_times(rows8):
    return jnp.concatenate([rows8] * 6, 0)


def summed(gathered_ref, first, last):
    total = gathered_ref[0, first:last, :]
    for s in range(1, SUB):
        total = total + gathered_ref[s, first:last, :]
    return total


def partner_places(names_ref, gathered_ref, sub):
    weights, columns = [], []
    high_rows = row_iota(24)
    low_rows = row_iota(LANES)
    for s in range(SUB):
        for j in range(4):
            names = gathered_ref[s, NAMES + j : NAMES + j + 1, :].astype(jnp.int32)
            row_hit = (names >> 7) == high_rows
            weights.append(
                jnp.concatenate(
                    [
                        jnp.where(row_hit, F32(4 * s + j), 0.0),
                        jnp.where(row_hit, lane_iota(24).astype(F32), 0.0),
                    ],
                    0,
                ).astype(BF16)
            )
            columns.append(jnp.where((names & 127) == low_rows, 1.0, 0.0).astype(BF16))
    table = lax.dot_general(
        jnp.concatenate(weights, 1),
        jnp.concatenate(columns, 1),
        (((1,), (1,)), ((), ())),
        preferred_element_type=F32,
    )
    chunks, lanes = [], []
    for j in range(4):
        name = names_ref[j : j + 1, :]
        low = jnp.broadcast_to(name & 127, (24, LANES))
        hit = high_rows == (name >> 7)
        chunk_sum = jnp.where(hit, take_lanes(table[:24], low), 0.0).sum(0, keepdims=True)
        lane_sum = jnp.where(hit, take_lanes(table[24:], low), 0.0).sum(0, keepdims=True)
        chunk = chunk_sum.astype(jnp.int32) - (4 * sub + j)
        lane = lane_sum.astype(jnp.int32) - lane_iota(1)
        below, above = name < RIM, name >= FACES_PART
        chunk = jnp.where(below, 4 * SUB, jnp.where(above, 4 * SUB + 1, chunk))
        lane = jnp.where(below | above, name & 127, lane)
        chunks.append(chunk)
        lanes.append(lane)
    return jnp.concatenate(chunks, 0), jnp.concatenate(lanes, 0) & 127


def face_values(names_ref, gathered_ref, up_list, loads_ref, shifts_ref):
    for j in range(4):
        name = names_ref[j : j + 1, :]
        high = jnp.broadcast_to(name >> 7, (24, LANES))
        low = jnp.broadcast_to(name & 127, (24, LANES))
        got = jnp.where(high == 0, take_lanes(up_list, low), 0.0)
        for s in range(SUB):
            for half in range(2):
                source = jnp.concatenate(
                    [
                        gathered_ref[s, LOADS + 12 * half : LOADS + 12 * half + 12, :],
                        gathered_ref[s, SHIFTS + 12 * half : SHIFTS + 12 * half + 12, :],
                    ],
                    0,
                )
                got = jnp.where(high == 2 * s + half + 1, take_lanes(source, low), got)
        loads_ref[pl.ds(j, FD, stride=4), :] = got[:FD]
        shifts_ref[pl.ds(j, FD, stride=4), :] = got[FD:]


def put_terms(terms, names_ref, own_ref, on_ref, off_ref, stage_ref, dom):
    whole, exponent = coded(terms)
    stage_ref[:NF, :] = whole
    stage_ref[NF:, :] = jnp.broadcast_to(exponent, (stage_ref.shape[0] - NF, LANES))
    own_ref[...] = as_sent(stage_ref[...])
    low, high = rim_lists(stage_ref, names_ref)
    put_lists(on_ref, off_ref, [high, spread_row(exponent)], [low, spread_row(exponent)], dom)


def second_kernel(
    inverse_ref, coupling_ref, trace_ref, names_ref, living_ref, sent_ref,
    chunk_ref, lane_ref, valid_ref, weight_ref, shifts_ref, view_ref, terms_ref, own_ref, on_ref, off_ref, inner_ref,
    loads_ref, stage_ref, gathered_ref,
):
    dom, sub = ids()
    count = lax.axis_size("dom")
    decode_first(sent_ref, gathered_ref)
    chunk, lane = partner_places(names_ref, gathered_ref, sub)
    chunk, lane = twice(chunk), twice(lane)
    names = twice(names_ref[...])
    valid = jnp.where((names < RIM) & (dom == 0), 0.0, 1.0)
    weight = jnp.where((names >= FACES_PART) & (dom == count - 1), 1.0, 0.5)
    chunk_ref[...] = chunk
    lane_ref[...] = lane
    valid_ref[...] = valid
    weight_ref[...] = weight
    up_list = jnp.concatenate(
        [summed(gathered_ref, UP, UP + FD), summed(gathered_ref, UP_SHIFT, UP_SHIFT + FD)], 0
    )
    down_list = summed(gathered_ref, DOWN, DOWN + FD)
    face_values(names_ref, gathered_ref, up_list, loads_ref, shifts_ref)
    own_load = jnp.where(six_times(names) < RIM, 0.0, loads_ref[...])
    partner = partner_terms(gathered_ref, chunk, lane, up_list[:FD], down_list)
    view = jnp.where(six_times(valid) > 0.0, own_load + (gathered_ref[sub, :NF, :] + partner), 0.0)
    view_ref[...] = view
    def keep(inner):
        inner_ref[...] = inner

    terms = element_operator(inverse_ref, coupling_ref, trace_ref, view, living_ref, keep)
    terms_ref[...] = terms
    put_terms(terms, names_ref, own_ref, on_ref, off_ref, stage_ref, dom)


def next_view(gathered_ref, chunk_ref, lane_ref, valid_ref, shifts_ref, view_ref, terms_ref):
    low_list = summed(gathered_ref, LATER_UP, LATER_UP + FD)
    high_list = summed(gathered_ref, LATER_DOWN, LATER_DOWN + FD)
    partner = partner_terms(gathered_ref, chunk_ref[...], lane_ref[...], low_list, high_list)
    image = terms_ref[...] + partner + shifts_ref[...] * view_ref[...]
    return jnp.where(six_times(valid_ref[...]) > 0.0, image, 0.0)


def third_kernel(
    inverse_ref, coupling_ref, trace_ref, names_ref, living_ref, sent_ref,
    chunk_ref, lane_ref, valid_ref, shifts_ref, view_ref, terms_ref, before_ref,
    new_view_ref, new_terms_ref, own_ref, on_ref, off_ref, inner_ref,
    stage_ref, gathered_ref,
):
    dom, _ = ids()
    decode_later(sent_ref, gathered_ref)
    view = next_view(gathered_ref, chunk_ref, lane_ref, valid_ref, shifts_ref, view_ref, terms_ref)
    new_view_ref[...] = view
    inner_ref[0] = before_ref[...]

    def keep(inner):
        inner_ref[1] = inner

    terms = element_operator(inverse_ref, coupling_ref, trace_ref, view, living_ref, keep)
    new_terms_ref[...] = terms
    put_terms(terms, names_ref, own_ref, on_ref, off_ref, stage_ref, dom)


def fourth_kernel(
    inverse_ref, coupling_ref, trace_ref, living_ref, sent_ref,
    chunk_ref, lane_ref, valid_ref, weight_ref, shifts_ref, first_view_ref, view_ref, terms_ref, before_ref,
    inner_hbm, sums_hbm,
    inner_ref, sums_ref, gathered_ref, sems,
):
    copies = [
        pltpu.make_async_copy(before_ref, inner_hbm.at[pl.ds(0, 2)], sems.at[0]),
        pltpu.make_async_copy(inner_ref, inner_hbm.at[2], sems.at[1]),
    ]
    copies[0].start()

    def keep(inner):
        inner_ref[...] = inner
        copies[1].start()

    decode_later(sent_ref, gathered_ref)
    first, second = first_view_ref[...], view_ref[...]
    third = next_view(gathered_ref, chunk_ref, lane_ref, valid_ref, shifts_ref, view_ref, terms_ref)
    last = element_operator(inverse_ref, coupling_ref, trace_ref, third, living_ref, keep)
    weight = six_times(weight_ref[...])
    last = last + weight * (shifts_ref[...] * third)
    views = (first, second, third)
    products = [weight * views[i] * views[j] for i in range(3) for j in range(i, 3)]
    products += [view * last for view in views]
    lane = lane_iota(1)
    sums = jnp.zeros((1, LANES), F32)
    for place, product in enumerate(products):
        total = product.reshape(6, 8, LANES).sum(0).sum(0, keepdims=True).sum(1, keepdims=True)
        sums = sums + jnp.where(lane == place, total, 0.0)
    sums_ref[...] = jnp.broadcast_to(sums, sums_ref.shape)
    send = pltpu.make_async_copy(sums_ref, sums_hbm, sems.at[2])
    send.start()
    for copy in copies:
        copy.wait()
    send.wait()


def owner_kernel(
    first_sent_ref, second_sent_ref, third_sent_ref, trace_load_hbm, shift_hbm, *rest,
):
    solved_hbm, inner_hbm = rest[:2]
    owned_ref, kept_ref, terms_ref, chosen_ref, first_ref, second_ref, third_ref = rest[2:9]
    trace_load_ref, shift_ref, sems = rest[9:]
    copies = [
        pltpu.make_async_copy(trace_load_hbm, trace_load_ref, sems.at[0]),
        pltpu.make_async_copy(shift_hbm, shift_ref, sems.at[1]),
        pltpu.make_async_copy(solved_hbm, kept_ref.at[0], sems.at[2]),
        pltpu.make_async_copy(inner_hbm, kept_ref.at[pl.ds(1, 3)], sems.at[3]),
    ]
    for copy in copies:
        copy.start()
    decode_first(first_sent_ref, first_ref)
    decode_later(second_sent_ref, second_ref)
    decode_later(third_sent_ref, third_ref)
    _, sub = ids()
    wanted = lax.broadcasted_iota(jnp.int32, (2 * RIM, LANES), 0) + (RIM + 2 * RIM * sub)
    sources = (first_ref, second_ref, third_ref)
    for s in range(SUB):
        for j in range(4):
            columns = slice((4 * s + j) * LANES, (4 * s + j + 1) * LANES)
            names = first_ref[s, NAMES + j : NAMES + j + 1, :].astype(jnp.int32)
            chosen_ref[:, columns] = jnp.where(wanted == names, 1.0, 0.0).astype(BF16)
            for v, source in enumerate(sources):
                part = source[s, pl.ds(j, FD, stride=4), :]
                part = jnp.concatenate([part, jnp.zeros((4, LANES), F32)], 0)
                for piece, value in enumerate(split3(part)):
                    first = 16 * (3 * v + piece)
                    terms_ref[first : first + 16, columns] = value
    sums = lax.dot_general(
        terms_ref[...], chosen_ref[...], (((1,), (1,)), ((), ())), preferred_element_type=F32
    )
    for copy in copies:
        copy.wait()
    last = sub == SUB - 1
    downs = (
        summed(first_ref, DOWN, DOWN + FD),
        summed(second_ref, LATER_DOWN, LATER_DOWN + FD),
        summed(third_ref, LATER_DOWN, LATER_DOWN + FD),
    )
    current = None
    for v in range(3):
        rows = [sums[48 * v + 16 * piece : 48 * v + 16 * piece + FD] for piece in range(3)]
        total = rows[0] + rows[1] + rows[2]
        down = jnp.concatenate(
            [jnp.zeros((FD, RIM), F32), jnp.where(last, downs[v], 0.0)], 1
        )
        total = total + down
        if v == 0:
            current = total + trace_load_ref[...]
        else:
            current = total + shift_ref[...] * current
        owned_ref[v] = current


def coefficients(sums):
    lane = lane_iota(1)

    def entry(place):
        return jnp.where(lane == place, sums, 0.0).sum(1, keepdims=True)

    table = {}
    place = 0
    for i in range(3):
        for j in range(i, 3):
            table[i, j] = table[j, i] = entry(place)
            place += 1
    for i in range(3):
        table[i, 3] = entry(place)
        place += 1

    def form(left, right):
        total = None
        for i, a in enumerate(left):
            for j, b in enumerate(right):
                if a is None or b is None:
                    continue
                term = a * b * table[i, j]
                total = term if total is None else total + term
        return total

    def combine(left, factor, right):
        merged = []
        for i in range(max(len(left), len(right))):
            a = left[i] if i < len(left) else None
            b = right[i] if i < len(right) else None
            if b is None:
                merged.append(a)
            else:
                merged.append(factor * b if a is None else a + factor * b)
        return merged

    one = jnp.ones((1, 1), F32)
    residual, direction, result = [one], [one], []
    norm = table[0, 0]
    for iteration in range(3):
        image = [None] + direction
        step = norm / form(direction, image)
        result = combine(result, step, direction)
        if iteration < 2:
            residual = combine(residual, -step, image)
            new_norm = form(residual, residual)
            direction = combine(residual, new_norm / norm, direction)
            norm = new_norm
    return result


def last_kernel(
    living_ref, all_sums_ref, inner_ref, owned_ref,
    traces_ref, interior_ref,
):
    sums = all_sums_ref[...].reshape(-1, 8, LANES).sum(0).sum(0, keepdims=True)
    a, b, c = coefficients(sums)
    traces_ref[...] = a * owned_ref[0] + b * owned_ref[1] + c * owned_ref[2]
    lifted = a * inner_ref[1] + b * inner_ref[2] + c * inner_ref[3]
    living = jnp.broadcast_to(living_ref[:1, :], (NI, LANES)) > 0.0
    interior_ref[...] = jnp.where(living, inner_ref[0] - lifted, 0.0)


def call(kernel, outputs, inputs, scratch=(), limit=6, from_hbm=(), to_hbm=()):
    held = [pltpu.with_memory_space_constraint(x, pltpu.HBM) for x in from_hbm]
    near, far = pl.BlockSpec(memory_space=pltpu.VMEM), pl.BlockSpec(memory_space=pltpu.HBM)
    return pl.pallas_call(
        kernel,
        out_shape=[jax.ShapeDtypeStruct(s, d) for s, d in outputs]
        + [pltpu.HBM(s, d) for s, d in to_hbm],
        in_specs=[near] * len(inputs) + [far] * len(held),
        out_specs=[near] * len(outputs) + [far] * len(to_hbm),
        scratch_shapes=list(scratch),
        compiler_params=pltpu.CompilerParams(vmem_limit_bytes=limit * MIB),
    )(*inputs, *held)


def to_all(blocks, rows):
    rest = rows - sum(len(block) for block in blocks)
    value = jnp.concatenate(blocks + [jnp.zeros((rest, LANES), I16)], 0)
    copies = jnp.broadcast_to(value[None], (SUB,) + value.shape)
    return lax.all_to_all(copies, "sub", 0, 0, tiled=True)


def neighbours(on, off):
    count = lax.axis_size("dom")
    pairs = [(i, i + 1) for i in range(1, count - 1, 2)]
    from_off = lax.ppermute(off, "dom", pairs + [(j, i) for i, j in pairs])
    from_on = lax.ppermute(on, "dom", [(i, i ^ 1) for i in range(count)])
    even = lax.axis_index("dom") % 2 == 0
    return jnp.where(even, from_off, from_on), jnp.where(even, from_on, from_off)


def later(own, on, off):
    from_below, from_above = neighbours(on, off)
    return to_all([own[:LATER_UP], from_below[: FD + 1], from_above[: FD + 1]], LATER_ROWS)


def on_device(
    interior_inverse, coupling, trace_block, interior_load, trace_load, face_shift, element_faces, block_padding,
):
    slab, rows8 = ((NF, LANES), F32), ((8, LANES), F32)
    places = ((8, LANES), jnp.int32)
    sent = [((64, LANES), I16), ((16, LANES), I16), ((16, LANES), I16)]
    stage = pltpu.VMEM((64, LANES), F32)
    decoded = pltpu.VMEM((SUB, LATER_ROWS, LANES), F32)
    decoded_first = pltpu.VMEM((SUB, FIRST_ROWS, LANES), F32)
    matrices = [interior_inverse, coupling, trace_block]

    inner = ((NI, LANES), F32)

    living, own, on, off, solved = call(
        first_kernel,
        [rows8, ((112, LANES), I16), ((32, LANES), I16), ((32, LANES), I16)],
        [],
        from_hbm=[
            interior_inverse, coupling, interior_load, trace_load, face_shift, element_faces,
            jnp.pad(block_padding, (0, LANES - 1))[None],
        ],
        to_hbm=[inner],
        scratch=[
            pltpu.VMEM((NI, LANES), F32), pltpu.VMEM((NI, NI, LANES), BF16), pltpu.VMEM((NI, NF, LANES), BF16),
            pltpu.VMEM((NI, LANES), BF16), pltpu.VMEM((FD, 2 * RIM), F32), pltpu.VMEM((FD, 2 * RIM), F32),
            pltpu.VMEM((4, LANES), jnp.int32), pltpu.VMEM((1, LANES), jnp.int32), pltpu.VMEM((112, LANES), F32),
            pltpu.SemaphoreType.DMA((PARTS + 7,)),
        ],
        limit=10,
    )
    from_below, from_above = neighbours(on, off)
    first = to_all([own[:UP], from_below[: DOWN - UP], from_above[: FD + 1]], FIRST_ROWS)
    chunk, lane, valid, weight, shifts, view0, terms, own, on, off, kept = call(
        second_kernel,
        [places, places, rows8, rows8, slab, slab, slab, *sent, inner],
        [*matrices, element_faces, living, first],
        scratch=[pltpu.VMEM((NF, LANES), F32), stage, decoded_first],
    )
    second = later(own, on, off)
    view1, terms1, own, on, off, kept = call(
        third_kernel,
        [slab, slab, *sent, ((2, NI, LANES), F32)],
        [*matrices, element_faces, living, second, chunk, lane, valid, shifts, view0, terms, kept],
        scratch=[stage, decoded],
    )
    third = later(own, on, off)
    everyone = lax.axis_size("dom") * SUB
    kept, sums = call(
        fourth_kernel,
        [],
        [*matrices, living, third, chunk, lane, valid, weight, shifts, view0, view1, terms1, kept],
        to_hbm=[((3, NI, LANES), F32), ((everyone, LANES), F32)],
        scratch=[
            pltpu.VMEM((NI, LANES), F32), pltpu.VMEM((everyone, LANES), F32), decoded,
            pltpu.SemaphoreType.DMA((3,)),
        ],
    )
    all_sums = lax.all_to_all(sums, ("dom", "sub"), 0, 0, tiled=True)
    owned, kept = call(
        owner_kernel,
        [((3, FD, 2 * RIM), F32), ((4, NI, LANES), F32)],
        [first, second, third],
        from_hbm=[trace_load, face_shift, solved, kept],
        scratch=[
            pltpu.VMEM((144, 32 * LANES), BF16), pltpu.VMEM((2 * RIM, 32 * LANES), BF16),
            decoded_first, decoded, decoded,
            pltpu.VMEM((FD, 2 * RIM), F32), pltpu.VMEM((FD, 2 * RIM), F32), pltpu.SemaphoreType.DMA((4,)),
        ],
        limit=14,
    )
    traces, interior = call(
        last_kernel,
        [((FD, 2 * RIM), F32), ((NI, LANES), F32)],
        [living, all_sums, kept, owned],
    )
    return traces, interior


def solution(mesh):
    last = ("dom", "sub")
    placed = (
        P(None, None, last), P(None, None, last), P(None, None, last),
        P(None, last), P(None, last), P(None, last), P(None, last), P(last),
    )
    return jax.shard_map(
        on_device,
        mesh=mesh,
        in_specs=placed,
        out_specs=(P(None, last), P(None, last)),
        check_vma=False,
    )
```

```python
import functools

import jax
import jax.numpy as jnp
from jax import lax
from jax.experimental import pallas as pl
from jax.experimental.pallas import tpu as pltpu
from jax.sharding import PartitionSpec as P

NI = 80
FD = 12
NF = 48
LANES = 128
RIM = 128
SUB = 8
FACES_PART = 2048
F32 = jnp.float32
BF16 = jnp.bfloat16
MIB = 1024 * 1024
PARTS = 5

I16 = jnp.int16

BIAS = 16384.0
SCALE_LANE = 64
PUSHED, LOADS, SHIFTS, NAMES, SCALES, UP, UP_SHIFT, DOWN, FIRST_END, FIRST_ROWS = (
    0, 48, 72, 96, 100, 103, 116, 129, 142, 144,
)
LATER_UP, LATER_DOWN, LATER_END, LATER_ROWS = 49, 62, 75, 80


def row_iota(rows):
    return lax.broadcasted_iota(jnp.int32, (rows, LANES), 0)


def lane_iota(rows):
    return lax.broadcasted_iota(jnp.int32, (rows, LANES), 1)


def eight_sums(parts):
    rows = row_iota(8)
    low = rows < 4
    parts = [
        jnp.where(low, parts[i], parts[i + 4])
        + pltpu.roll(jnp.where(low, parts[i + 4], parts[i]), 4, 0)
        for i in range(4)
    ]
    for step in (2, 1):
        low = (rows & step) == 0
        parts = [
            jnp.where(
                low,
                parts[i] + pltpu.roll(parts[i], 8 - step, 0),
                parts[i + step] + pltpu.roll(parts[i + step], step, 0),
            )
            for i in range(step)
        ]
    return parts[0]


def matrix_times(matrix_ref, vector):
    rows, depth, _ = matrix_ref.shape
    blocks = []
    for first in range(0, rows, 8):
        parts = [
            (matrix_ref[first + i].astype(F32) * vector)
            .reshape(depth // 8, 8, LANES)
            .sum(0)
            for i in range(8)
        ]
        blocks.append(eight_sums(parts))
    return jnp.concatenate(blocks, 0)


def transposed_times(matrix_ref, vector):
    depth = matrix_ref.shape[0]
    totals = [None, None]
    for i in range(depth):
        term = matrix_ref[i].astype(F32) * vector[i : i + 1]
        totals[i % 2] = term if totals[i % 2] is None else totals[i % 2] + term
    return totals[0] + totals[1]


def coded(value):
    top = jnp.abs(value).max(0, keepdims=True).max(1, keepdims=True)
    exponent = jnp.floor(jnp.log2(jnp.maximum(top, 2.0**-100))) + 1.0
    whole = jnp.floor(value * jnp.exp2(15.0 - exponent) + 0.5)
    return jnp.clip(whole, -32767.0, 32767.0), exponent


def spread_row(exponent):
    return jnp.broadcast_to(exponent + BIAS, (1, LANES))


def as_sent(value):
    return value.astype(jnp.int32).astype(I16)


def with_exponent(value):
    whole, exponent = coded(value)
    return [whole, spread_row(exponent)]


def put_lists(on_ref, off_ref, up, down, dom):
    even = dom % 2 == 0
    rest = [jnp.zeros((on_ref.shape[0] - sum(len(x) for x in up), LANES), F32)]
    up, down = jnp.concatenate(up + rest, 0), jnp.concatenate(down + rest, 0)
    on_ref[...] = as_sent(jnp.where(even, up, down))
    off_ref[...] = as_sent(jnp.where(even, down, up))


def decode(sent_ref, terms_ref, sections, scale_rows, least=None):
    rows = sent_ref.shape[1]
    row = row_iota(rows)
    for s in range(SUB):
        terms_ref[s] = sent_ref[s].astype(jnp.int32).astype(F32)
    base = least
    for s in range(SUB):
        for place in scale_rows:
            exponent = terms_ref[s, place : place + 1, :] - BIAS
            base = exponent if base is None else jnp.maximum(base, exponent)
    for s in range(SUB):
        factors = jnp.ones((1, LANES), F32)
        for end, exponent, scaled in reversed(sections):
            if exponent is None:
                factor = jnp.ones((1, LANES), F32)
            else:
                power = terms_ref[s, exponent : exponent + 1, :] - (BIAS + 15.0)
                factor = jnp.exp2(power - base if scaled else power)
            factors = jnp.where(row < end, factor, factors)
        terms_ref[s] = terms_ref[s] * factors
    return base


def decode_first(sent_ref, terms_ref):
    return decode(
        sent_ref,
        terms_ref,
        [
            (LOADS, SCALES, True), (SHIFTS, SCALES + 1, True), (NAMES, SCALES + 2, False), (UP, None, False),
            (UP + FD, UP + FD, True), (UP_SHIFT, None, False), (UP_SHIFT + FD, UP_SHIFT + FD, False),
            (DOWN, None, False), (FIRST_END, DOWN + FD, True),
        ],
        (SCALES, SCALES + 1, UP + FD, DOWN + FD),
    )


def decode_later(sent_ref, terms_ref, before):
    return decode(
        sent_ref,
        terms_ref,
        [
            (NF, NF, True), (LATER_UP, None, False), (LATER_UP + FD, LATER_UP + FD, True),
            (LATER_DOWN, None, False), (LATER_END, LATER_DOWN + FD, True),
        ],
        (NF, LATER_UP + FD, LATER_DOWN + FD),
        before + 3.0,
    )


def ids():
    return lax.axis_index("dom"), lax.axis_index("sub")


def element_operator(inverse_ref, coupling_ref, trace_ref, view, living_ref, keep):
    inner = matrix_times(inverse_ref, matrix_times(coupling_ref, view))
    keep(inner)
    terms = transposed_times(coupling_ref, inner) + matrix_times(trace_ref, view)
    return jnp.where(six_times(living_ref[...]) > 0.0, terms, 0.0)


def split3(value):
    high = value.astype(BF16)
    rest = value - high.astype(F32)
    middle = rest.astype(BF16)
    low = (rest - middle.astype(F32)).astype(BF16)
    return high, middle, low


def whole_pick(values, chosen):
    high = jnp.floor(values * (1.0 / 256.0))
    stacked = jnp.concatenate([high, values - 256.0 * high], 0).astype(BF16)
    sums = lax.dot_general(
        stacked, chosen, (((1,), (1,)), ((), ())), preferred_element_type=F32
    )
    rows = values.shape[0]
    return 256.0 * sums[:rows] + sums[rows:]


def face_major(terms_ref):
    slots = []
    for j in range(4):
        part = terms_ref[pl.ds(j, FD, stride=4), :]
        slots.append(jnp.concatenate([part, jnp.zeros((4, LANES), F32)], 0))
    return jnp.concatenate(slots, 1)


def rim_lists(terms_ref, names_ref):
    wanted = lax.broadcasted_iota(jnp.int32, (2 * RIM, LANES), 0)
    wanted = jnp.where(wanted < RIM, wanted, wanted + FACES_PART - RIM)
    chosen = [
        jnp.where(wanted == names_ref[j : j + 1, :], 1.0, 0.0).astype(BF16)
        for j in range(4)
    ]
    lists = whole_pick(face_major(terms_ref), jnp.concatenate(chosen, 1))
    return lists[:FD, :RIM], lists[:FD, RIM:]


def first_kernel(
    padding_ref, inverse_hbm, coupling_hbm, interior_load_hbm, trace_load_hbm, shift_hbm, names_hbm,
    living_ref, own_ref, on_ref, off_ref, solved_hbm,
    solved_ref, inverse_ref, coupling_ref, interior_load_ref, trace_load_ref, shift_ref, names_ref, stage_ref, sems,
):
    rows = NI // PARTS
    copies = [pltpu.make_async_copy(interior_load_hbm, interior_load_ref, sems.at[0])]
    for part in range(PARTS):
        block = pl.ds(part * rows, rows)
        copies.append(
            pltpu.make_async_copy(inverse_hbm.at[block], inverse_ref.at[block], sems.at[1 + part])
        )
    rest = [
        (coupling_hbm, coupling_ref), (names_hbm, names_ref),
        (trace_load_hbm, trace_load_ref), (shift_hbm, shift_ref),
    ]
    for place, (source, target) in enumerate(rest):
        copies.append(pltpu.make_async_copy(source, target, sems.at[1 + PARTS + place]))
    for copy in copies:
        copy.start()
    dom, sub = ids()
    for copy in copies[2 + PARTS :]:
        copy.wait()
    living = lane_iota(1) < LANES - padding_ref[0]
    living_ref[...] = jnp.broadcast_to(jnp.where(living, 1.0, 0.0), (8, LANES))
    stage_ref[NAMES:, :] = jnp.zeros((stage_ref.shape[0] - NAMES, LANES), F32)
    loads, load_exponent = coded(trace_load_ref[...])
    shifts, shift_exponent = coded(shift_ref[...])
    for half in range(2):
        columns = slice(half * RIM, half * RIM + RIM)
        stage_ref[LOADS + FD * half : LOADS + FD * half + FD, :] = loads[:, columns]
        stage_ref[SHIFTS + FD * half : SHIFTS + FD * half + FD, :] = shifts[:, columns]
    stage_ref[NAMES : NAMES + 4, :] = names_ref[...].astype(F32)
    stage_ref[SCALES + 1 : SCALES + 2, :] = spread_row(load_exponent)
    stage_ref[SCALES + 2 : SCALES + 3, :] = spread_row(shift_exponent)
    copies[0].wait()
    load = interior_load_ref[...].astype(F32)
    solved = []
    for part in range(PARTS):
        copies[1 + part].wait()
        solved.append(matrix_times(inverse_ref.at[pl.ds(part * rows, rows)], load))
    solved = jnp.concatenate(solved, 0)
    solved_ref[...] = solved
    keep = pltpu.make_async_copy(solved_ref, solved_hbm, sems.at[PARTS + 5])
    keep.start()
    copies[1 + PARTS].wait()
    whole, exponent = coded(jnp.where(living, transposed_times(coupling_ref, solved), 0.0))
    stage_ref[:NF, :] = whole
    stage_ref[SCALES : SCALES + 1, :] = spread_row(exponent)
    low, high = rim_lists(stage_ref, names_ref)
    owner = sub == SUB - 1
    up = with_exponent(
        high * jnp.exp2(exponent - 15.0) + jnp.where(owner, trace_load_ref[:, RIM:], 0.0)
    )
    up += [jnp.where(owner, shifts[:, RIM:], 0.0), spread_row(shift_exponent)]
    down = [low, spread_row(exponent), jnp.zeros((FD + 1, LANES), F32)]
    put_lists(on_ref, off_ref, up, down, dom)
    own_ref[...] = as_sent(stage_ref[...])
    keep.wait()


def spread_rows(values, block):
    a = jnp.broadcast_to(values[2 * block : 2 * block + 1], (8, LANES))
    b = jnp.broadcast_to(values[2 * block + 1 : 2 * block + 2], (8, LANES))
    return jnp.where(row_iota(8) < 4, a, b)


def turn(values, steps):
    if steps == 0:
        return values
    rows = row_iota(8) & 3
    return jnp.where(
        rows < 4 - steps, pltpu.roll(values, 8 - steps, 0), pltpu.roll(values, 4 - steps, 0)
    )


def take_lanes(values, lanes):
    return jnp.take_along_axis(values, lanes, axis=1, mode="promise_in_bounds")


def partner_terms(gathered_ref, chunk, lane, low_list, high_list):
    rows = row_iota(8) & 3
    found = [jnp.zeros((8, LANES), F32) for _ in range(6)]
    for t in range(4):
        chunk_t = turn(chunk, (4 - t) % 4)
        lane_t = turn(lane, (4 - t) % 4)
        part = [jnp.zeros((8, LANES), F32) for _ in range(6)]
        for s in range(SUB):
            here = chunk_t == 4 * s + rows
            for g in range(6):
                taken = take_lanes(gathered_ref[s, 8 * g : 8 * g + 8, :], lane_t)
                part[g] = jnp.where(here, taken, part[g])
        for g in range(6):
            found[g] = found[g] + turn(part[g], t)
    on_low = chunk == 4 * SUB
    on_high = chunk == 4 * SUB + 1
    for g in range(6):
        found[g] = jnp.where(on_low, take_lanes(spread_rows(low_list, g), lane), found[g])
        found[g] = jnp.where(on_high, take_lanes(spread_rows(high_list, g), lane), found[g])
    return jnp.concatenate(found, 0)


def twice(slots):
    return jnp.concatenate([slots, slots], 0)


def six_times(rows8):
    return jnp.concatenate([rows8] * 6, 0)


def summed(gathered_ref, first, last):
    total = gathered_ref[0, first:last, :]
    for s in range(1, SUB):
        total = total + gathered_ref[s, first:last, :]
    return total


def partner_places(names_ref, gathered_ref, sub):
    weights, columns = [], []
    high_rows = row_iota(24)
    low_rows = row_iota(LANES)
    for s in range(SUB):
        for j in range(4):
            names = gathered_ref[s, NAMES + j : NAMES + j + 1, :].astype(jnp.int32)
            row_hit = (names >> 7) == high_rows
            weights.append(
                jnp.concatenate(
                    [
                        jnp.where(row_hit, F32(4 * s + j), 0.0),
                        jnp.where(row_hit, lane_iota(24).astype(F32), 0.0),
                    ],
                    0,
                ).astype(BF16)
            )
            columns.append(jnp.where((names & 127) == low_rows, 1.0, 0.0).astype(BF16))
    table = lax.dot_general(
        jnp.concatenate(weights, 1),
        jnp.concatenate(columns, 1),
        (((1,), (1,)), ((), ())),
        preferred_element_type=F32,
    )
    chunks, lanes = [], []
    for j in range(4):
        name = names_ref[j : j + 1, :]
        low = jnp.broadcast_to(name & 127, (24, LANES))
        hit = high_rows == (name >> 7)
        chunk_sum = jnp.where(hit, take_lanes(table[:24], low), 0.0).sum(0, keepdims=True)
        lane_sum = jnp.where(hit, take_lanes(table[24:], low), 0.0).sum(0, keepdims=True)
        chunk = chunk_sum.astype(jnp.int32) - (4 * sub + j)
        lane = lane_sum.astype(jnp.int32) - lane_iota(1)
        below, above = name < RIM, name >= FACES_PART
        chunk = jnp.where(below, 4 * SUB, jnp.where(above, 4 * SUB + 1, chunk))
        lane = jnp.where(below | above, name & 127, lane)
        chunks.append(chunk)
        lanes.append(lane)
    return jnp.concatenate(chunks, 0), jnp.concatenate(lanes, 0) & 127


def face_values(names_ref, gathered_ref, up_list, loads_ref, shifts_ref):
    for j in range(4):
        name = names_ref[j : j + 1, :]
        high = jnp.broadcast_to(name >> 7, (24, LANES))
        low = jnp.broadcast_to(name & 127, (24, LANES))
        got = jnp.where(high == 0, take_lanes(up_list, low), 0.0)
        for s in range(SUB):
            for half in range(2):
                source = jnp.concatenate(
                    [
                        gathered_ref[s, LOADS + 12 * half : LOADS + 12 * half + 12, :],
                        gathered_ref[s, SHIFTS + 12 * half : SHIFTS + 12 * half + 12, :],
                    ],
                    0,
                )
                got = jnp.where(high == 2 * s + half + 1, take_lanes(source, low), got)
        loads_ref[pl.ds(j, FD, stride=4), :] = got[:FD]
        shifts_ref[pl.ds(j, FD, stride=4), :] = got[FD:]


def put_terms(terms, base, names_ref, own_ref, on_ref, off_ref, stage_ref, dom):
    whole, exponent = coded(terms)
    exponent = exponent + base
    stage_ref[:NF, :] = whole
    stage_ref[NF:, :] = jnp.broadcast_to(exponent + BIAS, (stage_ref.shape[0] - NF, LANES))
    own_ref[...] = as_sent(stage_ref[...])
    low, high = rim_lists(stage_ref, names_ref)
    put_lists(on_ref, off_ref, [high, spread_row(exponent)], [low, spread_row(exponent)], dom)


def second_kernel(
    inverse_ref, coupling_ref, trace_ref, names_ref, living_ref, sent_ref,
    chunk_ref, lane_ref, valid_ref, weight_ref, shifts_ref, view_ref, terms_ref, own_ref, on_ref, off_ref, inner_ref, scale_ref,
    loads_ref, stage_ref, gathered_ref,
):
    dom, sub = ids()
    count = lax.axis_size("dom")
    base = decode_first(sent_ref, gathered_ref)
    scale_ref[...] = jnp.broadcast_to(base, (8, LANES))
    chunk, lane = partner_places(names_ref, gathered_ref, sub)
    chunk, lane = twice(chunk), twice(lane)
    names = twice(names_ref[...])
    valid = jnp.where((names < RIM) & (dom == 0), 0.0, 1.0)
    weight = jnp.where((names >= FACES_PART) & (dom == count - 1), 1.0, 0.5)
    chunk_ref[...] = chunk
    lane_ref[...] = lane
    valid_ref[...] = valid
    weight_ref[...] = weight
    up_list = jnp.concatenate(
        [summed(gathered_ref, UP, UP + FD), summed(gathered_ref, UP_SHIFT, UP_SHIFT + FD)], 0
    )
    down_list = summed(gathered_ref, DOWN, DOWN + FD)
    face_values(names_ref, gathered_ref, up_list, loads_ref, shifts_ref)
    own_load = jnp.where(six_times(names) < RIM, 0.0, loads_ref[...])
    partner = partner_terms(gathered_ref, chunk, lane, up_list[:FD], down_list)
    view = jnp.where(six_times(valid) > 0.0, own_load + (gathered_ref[sub, :NF, :] + partner), 0.0)
    view_ref[...] = view
    def keep(inner):
        inner_ref[...] = inner

    terms = element_operator(inverse_ref, coupling_ref, trace_ref, view, living_ref, keep)
    terms_ref[...] = terms
    put_terms(terms, base, names_ref, own_ref, on_ref, off_ref, stage_ref, dom)


def next_view(factor, gathered_ref, chunk_ref, lane_ref, valid_ref, shifts_ref, view_ref, terms_ref):
    low_list = summed(gathered_ref, LATER_UP, LATER_UP + FD)
    high_list = summed(gathered_ref, LATER_DOWN, LATER_DOWN + FD)
    partner = partner_terms(gathered_ref, chunk_ref[...], lane_ref[...], low_list, high_list)
    image = factor * (terms_ref[...] + shifts_ref[...] * view_ref[...]) + partner
    return jnp.where(six_times(valid_ref[...]) > 0.0, image, 0.0)


def third_kernel(
    inverse_ref, coupling_ref, trace_ref, names_ref, living_ref, sent_ref,
    chunk_ref, lane_ref, valid_ref, shifts_ref, view_ref, terms_ref, scale_ref, before_ref,
    new_view_ref, new_terms_ref, own_ref, on_ref, off_ref, inner_ref, new_scale_ref,
    stage_ref, gathered_ref,
):
    dom, _ = ids()
    scale = scale_ref[:1, :]
    base = decode_later(sent_ref, gathered_ref, scale)
    new_scale_ref[...] = jnp.where(row_iota(8) == 0, scale, base)
    factor = jnp.exp2(scale - base)
    view = next_view(factor, gathered_ref, chunk_ref, lane_ref, valid_ref, shifts_ref, view_ref, terms_ref)
    new_view_ref[...] = view
    inner_ref[0] = before_ref[...]

    def keep(inner):
        inner_ref[1] = inner

    terms = element_operator(inverse_ref, coupling_ref, trace_ref, view, living_ref, keep)
    new_terms_ref[...] = terms
    put_terms(terms, base, names_ref, own_ref, on_ref, off_ref, stage_ref, dom)


def fourth_kernel(
    inverse_ref, coupling_ref, trace_ref, living_ref, sent_ref,
    chunk_ref, lane_ref, valid_ref, weight_ref, shifts_ref, first_view_ref, view_ref, terms_ref, scale_ref, before_ref,
    inner_hbm, sums_hbm,
    inner_ref, sums_ref, gathered_ref, sems,
):
    copies = [
        pltpu.make_async_copy(before_ref, inner_hbm.at[pl.ds(0, 2)], sems.at[0]),
        pltpu.make_async_copy(inner_ref, inner_hbm.at[2], sems.at[1]),
    ]
    copies[0].start()

    def keep(inner):
        inner_ref[...] = inner
        copies[1].start()

    scales = [scale_ref[:1, :], scale_ref[1:2, :]]
    scales.append(decode_later(sent_ref, gathered_ref, scales[1]))
    factor = jnp.exp2(scales[1] - scales[2])
    first, second = first_view_ref[...], view_ref[...]
    third = next_view(factor, gathered_ref, chunk_ref, lane_ref, valid_ref, shifts_ref, view_ref, terms_ref)
    last = element_operator(inverse_ref, coupling_ref, trace_ref, third, living_ref, keep)
    weight = six_times(weight_ref[...])
    last = last + weight * (shifts_ref[...] * third)
    views = (first, second, third)
    weighted = [weight * view for view in views]
    products = [weighted[i] * views[j] for i in range(3) for j in range(i, 3)]
    products += [view * last for view in views]
    powers = [scales[i] + scales[j] for i in range(3) for j in range(i, 3)]
    powers += [scale + scales[2] for scale in scales]
    lane = lane_iota(1)
    sums = jnp.zeros((1, LANES), F32)
    for place, product in enumerate(products):
        sums = sums + jnp.where(lane == SCALE_LANE + place, powers[place], 0.0)
        total = product.reshape(6, 8, LANES).sum(0).sum(0, keepdims=True).sum(1, keepdims=True)
        sums = sums + jnp.where(lane == place, total, 0.0)
    sums_ref[...] = jnp.broadcast_to(sums, sums_ref.shape)
    send = pltpu.make_async_copy(sums_ref, sums_hbm, sems.at[2])
    send.start()
    for copy in copies:
        copy.wait()
    send.wait()


def owner_kernel(
    first_sent_ref, second_sent_ref, third_sent_ref, trace_load_hbm, shift_hbm, *rest,
):
    solved_hbm, inner_hbm = rest[:2]
    owned_ref, kept_ref, terms_ref, chosen_ref, first_ref, second_ref, third_ref = rest[2:9]
    trace_load_ref, shift_ref, sems = rest[9:]
    copies = [
        pltpu.make_async_copy(trace_load_hbm, trace_load_ref, sems.at[0]),
        pltpu.make_async_copy(shift_hbm, shift_ref, sems.at[1]),
        pltpu.make_async_copy(solved_hbm, kept_ref.at[0], sems.at[2]),
        pltpu.make_async_copy(inner_hbm, kept_ref.at[pl.ds(1, 3)], sems.at[3]),
    ]
    for copy in copies:
        copy.start()
    scales = [decode_first(first_sent_ref, first_ref)]
    scales.append(decode_later(second_sent_ref, second_ref, scales[0]))
    scales.append(decode_later(third_sent_ref, third_ref, scales[1]))
    _, sub = ids()
    wanted = lax.broadcasted_iota(jnp.int32, (2 * RIM, LANES), 0) + (RIM + 2 * RIM * sub)
    sources = (first_ref, second_ref, third_ref)
    for s in range(SUB):
        for j in range(4):
            columns = slice((4 * s + j) * LANES, (4 * s + j + 1) * LANES)
            names = first_ref[s, NAMES + j : NAMES + j + 1, :].astype(jnp.int32)
            chosen_ref[:, columns] = jnp.where(wanted == names, 1.0, 0.0).astype(BF16)
            for v, source in enumerate(sources):
                part = source[s, pl.ds(j, FD, stride=4), :]
                part = jnp.concatenate([part, jnp.zeros((4, LANES), F32)], 0)
                for piece, value in enumerate(split3(part)):
                    first = 16 * (3 * v + piece)
                    terms_ref[first : first + 16, columns] = value
    sums = lax.dot_general(
        terms_ref[...], chosen_ref[...], (((1,), (1,)), ((), ())), preferred_element_type=F32
    )
    for copy in copies:
        copy.wait()
    last = sub == SUB - 1
    downs = (
        summed(first_ref, DOWN, DOWN + FD),
        summed(second_ref, LATER_DOWN, LATER_DOWN + FD),
        summed(third_ref, LATER_DOWN, LATER_DOWN + FD),
    )
    current = None
    for v in range(3):
        rows = [sums[48 * v + 16 * piece : 48 * v + 16 * piece + FD] for piece in range(3)]
        total = rows[0] + rows[1] + rows[2]
        down = jnp.concatenate(
            [jnp.zeros((FD, RIM), F32), jnp.where(last, downs[v], 0.0)], 1
        )
        total = total + down
        if v == 0:
            current = total + jnp.exp2(-scales[0][:, :1]) * trace_load_ref[...]
        else:
            factor = jnp.exp2(scales[v - 1] - scales[v])[:, :1]
            current = total + factor * (shift_ref[...] * current)
        owned_ref[v] = current


def coefficients(sums, powers, own_powers):
    lane = lane_iota(1)

    def entry(row, place):
        return jnp.where(lane == place, row, 0.0).sum(1, keepdims=True)

    pairs = [(i, j) for i in range(3) for j in range(i, 3)]
    pairs += [(i, 3) for i in range(3)]
    places = [pairs.index((i, i)) for i in range(3)]
    scales = [0.5 * entry(powers, place) for place in places]
    own_scales = [0.5 * entry(own_powers, place) for place in places]
    table = {}
    for place, (i, j) in enumerate(pairs):
        power = entry(powers, place) - scales[i] - scales[min(j, 2)]
        table[i, j] = table[j, i] = entry(sums, place) * jnp.exp2(power)
    steps = [jnp.exp2(scales[1] - scales[0]), jnp.exp2(scales[2] - scales[1]), 1.0]

    def form(left, right):
        total = None
        for i, a in enumerate(left):
            for j, b in enumerate(right):
                if a is None or b is None:
                    continue
                term = a * b * table[i, j]
                total = term if total is None else total + term
        return total

    def combine(left, factor, right):
        merged = []
        for i in range(max(len(left), len(right))):
            a = left[i] if i < len(left) else None
            b = right[i] if i < len(right) else None
            if b is None:
                merged.append(a)
            else:
                merged.append(factor * b if a is None else a + factor * b)
        return merged

    one = jnp.ones((1, 1), F32)
    residual, direction, result = [one], [one], []
    norm = table[0, 0]
    for iteration in range(3):
        image = [None] + [a * b for a, b in zip(direction, steps, strict=False)]
        step = norm / form(direction, image)
        result = combine(result, step, direction)
        if iteration < 2:
            residual = combine(residual, -step, image)
            new_norm = form(residual, residual)
            direction = combine(residual, new_norm / norm, direction)
            norm = new_norm
    return [
        part * jnp.exp2(scales[0] - scale + own)
        for part, scale, own in zip(result, scales, own_scales, strict=True)
    ]


def last_kernel(
    living_ref, all_sums_ref, inner_ref, owned_ref,
    traces_ref, interior_ref,
):
    dom, sub = ids()
    sums = all_sums_ref[...]
    powers = pltpu.roll(sums, LANES - SCALE_LANE, 1)
    own = pltpu.roll(all_sums_ref[pl.ds(dom * SUB + sub, 1), :], LANES - SCALE_LANE, 1)
    used = lane_iota(1) < SCALE_LANE
    powers, own = jnp.where(used, powers, 0.0), jnp.where(used, own, 0.0)
    top = powers.reshape(-1, 8, LANES).max(0).max(0, keepdims=True)
    sums = (sums * jnp.exp2(powers - top)).reshape(-1, 8, LANES).sum(0).sum(0, keepdims=True)
    a, b, c = coefficients(sums, top, own)
    traces_ref[...] = a * owned_ref[0] + b * owned_ref[1] + c * owned_ref[2]
    lifted = a * inner_ref[1] + b * inner_ref[2] + c * inner_ref[3]
    living = jnp.broadcast_to(living_ref[:1, :], (NI, LANES)) > 0.0
    interior_ref[...] = jnp.where(living, inner_ref[0] - lifted, 0.0)


def call(kernel, outputs, inputs, scratch=(), limit=6, from_hbm=(), to_hbm=()):
    held = [pltpu.with_memory_space_constraint(x, pltpu.HBM) for x in from_hbm]
    near, far = pl.BlockSpec(memory_space=pltpu.VMEM), pl.BlockSpec(memory_space=pltpu.HBM)
    return pl.pallas_call(
        kernel,
        out_shape=[jax.ShapeDtypeStruct(s, d) for s, d in outputs]
        + [pltpu.HBM(s, d) for s, d in to_hbm],
        in_specs=[near if x.ndim > 1 else pl.BlockSpec(memory_space=pltpu.SMEM) for x in inputs]
        + [far] * len(held),
        out_specs=[near] * len(outputs) + [far] * len(to_hbm),
        scratch_shapes=list(scratch),
        compiler_params=pltpu.CompilerParams(vmem_limit_bytes=limit * MIB),
    )(*inputs, *held)


def to_all(blocks, rows):
    rest = rows - sum(len(block) for block in blocks)
    value = jnp.concatenate(blocks + [jnp.zeros((rest, LANES), I16)], 0)
    copies = jnp.broadcast_to(value[None], (SUB,) + value.shape)
    return lax.all_to_all(copies, "sub", 0, 0, tiled=True)


def neighbours(on, off):
    count = lax.axis_size("dom")
    pairs = [(i, i + 1) for i in range(1, count - 1, 2)]
    from_off = lax.ppermute(off, "dom", pairs + [(j, i) for i, j in pairs])
    from_on = lax.ppermute(on, "dom", [(i, i ^ 1) for i in range(count)])
    even = lax.axis_index("dom") % 2 == 0
    return jnp.where(even, from_off, from_on), jnp.where(even, from_on, from_off)


def later(own, on, off):
    from_below, from_above = neighbours(on, off)
    return to_all([own[:LATER_UP], from_below[: FD + 1], from_above[: FD + 1]], LATER_ROWS)


def on_device(
    interior_inverse, coupling, trace_block, interior_load, trace_load, face_shift, element_faces, block_padding,
):
    slab, rows8 = ((NF, LANES), F32), ((8, LANES), F32)
    places = ((8, LANES), jnp.int32)
    sent = [((64, LANES), I16), ((16, LANES), I16), ((16, LANES), I16)]
    stage = pltpu.VMEM((64, LANES), F32)
    decoded = pltpu.VMEM((SUB, LATER_ROWS, LANES), F32)
    decoded_first = pltpu.VMEM((SUB, FIRST_ROWS, LANES), F32)
    matrices = [interior_inverse, coupling, trace_block]

    inner = ((NI, LANES), F32)

    living, own, on, off, solved = call(
        first_kernel,
        [rows8, ((112, LANES), I16), ((32, LANES), I16), ((32, LANES), I16)],
        [block_padding],
        from_hbm=[interior_inverse, coupling, interior_load, trace_load, face_shift, element_faces],
        to_hbm=[inner],
        scratch=[
            pltpu.VMEM((NI, LANES), F32), pltpu.VMEM((NI, NI, LANES), BF16), pltpu.VMEM((NI, NF, LANES), BF16),
            pltpu.VMEM((NI, LANES), BF16), pltpu.VMEM((FD, 2 * RIM), F32), pltpu.VMEM((FD, 2 * RIM), F32),
            pltpu.VMEM((4, LANES), jnp.int32), pltpu.VMEM((112, LANES), F32),
            pltpu.SemaphoreType.DMA((PARTS + 6,)),
        ],
        limit=10,
    )
    from_below, from_above = neighbours(on, off)
    first = to_all([own[:UP], from_below[: DOWN - UP], from_above[: FD + 1]], FIRST_ROWS)
    chunk, lane, valid, weight, shifts, view0, terms, own, on, off, kept, scale = call(
        second_kernel,
        [places, places, rows8, rows8, slab, slab, slab, *sent, inner, rows8],
        [*matrices, element_faces, living, first],
        scratch=[pltpu.VMEM((NF, LANES), F32), stage, decoded_first],
    )
    second = later(own, on, off)
    view1, terms1, own, on, off, kept, scale = call(
        third_kernel,
        [slab, slab, *sent, ((2, NI, LANES), F32), rows8],
        [*matrices, element_faces, living, second, chunk, lane, valid, shifts, view0, terms, scale, kept],
        scratch=[stage, decoded],
    )
    third = later(own, on, off)
    everyone = lax.axis_size("dom") * SUB
    kept, sums = call(
        fourth_kernel,
        [],
        [*matrices, living, third, chunk, lane, valid, weight, shifts, view0, view1, terms1, scale, kept],
        to_hbm=[((3, NI, LANES), F32), ((everyone, LANES), F32)],
        scratch=[
            pltpu.VMEM((NI, LANES), F32), pltpu.VMEM((everyone, LANES), F32), decoded,
            pltpu.SemaphoreType.DMA((3,)),
        ],
    )
    all_sums = lax.all_to_all(sums, ("dom", "sub"), 0, 0, tiled=True)
    owned, kept = call(
        owner_kernel,
        [((3, FD, 2 * RIM), F32), ((4, NI, LANES), F32)],
        [first, second, third],
        from_hbm=[trace_load, face_shift, solved, kept],
        scratch=[
            pltpu.VMEM((144, 32 * LANES), BF16), pltpu.VMEM((2 * RIM, 32 * LANES), BF16),
            decoded_first, decoded, decoded,
            pltpu.VMEM((FD, 2 * RIM), F32), pltpu.VMEM((FD, 2 * RIM), F32), pltpu.SemaphoreType.DMA((4,)),
        ],
        limit=14,
    )
    traces, interior = call(
        last_kernel,
        [((FD, 2 * RIM), F32), ((NI, LANES), F32)],
        [living, all_sums, kept, owned],
    )
    return traces, interior


def solution(mesh):
    last = ("dom", "sub")
    placed = (
        P(None, None, last), P(None, None, last), P(None, None, last),
        P(None, last), P(None, last), P(None, last), P(None, last), P(last),
    )
    return jax.shard_map(
        on_device,
        mesh=mesh,
        in_specs=placed,
        out_specs=(P(None, last), P(None, last)),
        check_vma=False,
    )
```

```python
import functools

import jax
import jax.numpy as jnp
from jax import lax
from jax.experimental import pallas as pl
from jax.experimental.pallas import tpu as pltpu
from jax.sharding import PartitionSpec as P

NI = 80
FD = 12
NF = 48
LANES = 128
RIM = 128
SUB = 8
FACES_PART = 2048
F32 = jnp.float32
BF16 = jnp.bfloat16
MIB = 1024 * 1024
PARTS = 5

I16 = jnp.int16

BIAS = 16384.0
SCALE_LANE = 64
FACES, NAMES, SCALES, UP, UP_SHIFT, DOWN, FIRST_ROWS = 48, 96, 100, 105, 118, 131, 144
LATER_UP, LATER_DOWN, LATER_ROWS = 54, 67, 80


def row_iota(rows):
    return lax.broadcasted_iota(jnp.int32, (rows, LANES), 0)


def lane_iota(rows):
    return lax.broadcasted_iota(jnp.int32, (rows, LANES), 1)


def eight_sums(parts):
    rows = row_iota(8)
    low = rows < 4
    parts = [
        jnp.where(low, parts[i], parts[i + 4])
        + pltpu.roll(jnp.where(low, parts[i + 4], parts[i]), 4, 0)
        for i in range(4)
    ]
    for step in (2, 1):
        low = (rows & step) == 0
        parts = [
            jnp.where(
                low,
                parts[i] + pltpu.roll(parts[i], 8 - step, 0),
                parts[i + step] + pltpu.roll(parts[i + step], step, 0),
            )
            for i in range(step)
        ]
    return parts[0]


def matrix_times(matrix_ref, vector):
    rows, depth, _ = matrix_ref.shape
    blocks = []
    for first in range(0, rows, 8):
        parts = [
            (matrix_ref[first + i].astype(F32) * vector)
            .reshape(depth // 8, 8, LANES)
            .sum(0)
            for i in range(8)
        ]
        blocks.append(eight_sums(parts))
    return jnp.concatenate(blocks, 0)


def transposed_times(matrix_ref, vector):
    depth = matrix_ref.shape[0]
    totals = [None, None]
    for i in range(depth):
        term = matrix_ref[i].astype(F32) * vector[i : i + 1]
        totals[i % 2] = term if totals[i % 2] is None else totals[i % 2] + term
    return totals[0] + totals[1]


def coded(value):
    top = jnp.abs(value).max(0, keepdims=True).max(1, keepdims=True)
    exponent = jnp.floor(jnp.log2(jnp.maximum(top, 2.0**-100))) + 1.0
    whole = jnp.floor(value * jnp.exp2(15.0 - exponent) + 0.5)
    return jnp.clip(whole, -32767.0, 32767.0), exponent


def spread_row(exponent):
    return jnp.broadcast_to(exponent + BIAS, (1, LANES))


def as_sent(value):
    return value.astype(jnp.int32).astype(I16)


def with_exponent(value):
    whole, exponent = coded(value)
    return [whole, spread_row(exponent)]


def put_lists(on_ref, off_ref, up, down, dom):
    even = dom % 2 == 0
    rest = [jnp.zeros((on_ref.shape[0] - sum(len(x) for x in up), LANES), F32)]
    up, down = jnp.concatenate(up + rest, 0), jnp.concatenate(down + rest, 0)
    on_ref[...] = as_sent(jnp.where(even, up, down))
    off_ref[...] = as_sent(jnp.where(even, down, up))


def decode(sent_ref, terms_ref, sections, scale_rows, least=None):
    rows = sent_ref.shape[1]
    row = row_iota(rows)
    for s in range(SUB):
        terms_ref[s] = sent_ref[s].astype(jnp.int32).astype(F32)
    base = least
    for s in range(SUB):
        for place in scale_rows:
            exponent = terms_ref[s, place : place + 1, :] - BIAS
            base = exponent if base is None else jnp.maximum(base, exponent)
    for s in range(SUB):
        factors = jnp.ones((1, LANES), F32)
        for end, exponent, scaled in reversed(sections):
            if exponent is None:
                factor = jnp.ones((1, LANES), F32)
            else:
                power = terms_ref[s, exponent : exponent + 1, :] - (BIAS + 15.0)
                factor = jnp.exp2(power - base if scaled else power)
            factors = jnp.where(row < end, factor, factors)
        terms_ref[s] = terms_ref[s] * factors
    return base


def decode_first(sent_ref, terms_ref):
    return decode(
        sent_ref,
        terms_ref,
        [
            (FACES, SCALES, True), (FACES + FD, SCALES + 1, True), (FACES + 2 * FD, SCALES + 2, False),
            (FACES + 3 * FD, SCALES + 1, True), (NAMES, SCALES + 2, False), (UP, None, False),
            (UP + FD, UP + FD, True), (UP_SHIFT, None, False), (UP_SHIFT + FD, UP_SHIFT + FD, False),
            (DOWN, None, False), (FIRST_ROWS, DOWN + FD, True),
        ],
        (SCALES, SCALES + 1, UP + FD, DOWN + FD),
    )


def decode_later(sent_ref, terms_ref, before):
    return decode(
        sent_ref,
        terms_ref,
        [
            (NF, NF, True), (LATER_UP, None, False), (LATER_UP + FD, LATER_UP + FD, True),
            (LATER_DOWN, None, False), (LATER_ROWS, LATER_DOWN + FD, True),
        ],
        (NF, LATER_UP + FD, LATER_DOWN + FD),
        before + 3.0,
    )


def ids():
    return lax.axis_index("dom"), lax.axis_index("sub")


def element_operator(inverse_ref, coupling_ref, trace_ref, view, living_ref, keep):
    inner = matrix_times(inverse_ref, matrix_times(coupling_ref, view))
    keep(inner)
    terms = transposed_times(coupling_ref, inner) + matrix_times(trace_ref, view)
    return jnp.where(six_times(living_ref[...]) > 0.0, terms, 0.0)


def split3(value):
    high = value.astype(BF16)
    rest = value - high.astype(F32)
    middle = rest.astype(BF16)
    low = (rest - middle.astype(F32)).astype(BF16)
    return high, middle, low


def whole_pick(values, chosen):
    high = jnp.floor(values * (1.0 / 256.0))
    stacked = jnp.concatenate([high, values - 256.0 * high], 0).astype(BF16)
    sums = lax.dot_general(
        stacked, chosen, (((1,), (1,)), ((), ())), preferred_element_type=F32
    )
    rows = values.shape[0]
    return 256.0 * sums[:rows] + sums[rows:]


def face_major(terms_ref):
    slots = []
    for j in range(4):
        part = terms_ref[pl.ds(j, FD, stride=4), :]
        slots.append(jnp.concatenate([part, jnp.zeros((4, LANES), F32)], 0))
    return jnp.concatenate(slots, 1)


def rim_lists(terms_ref, names_ref):
    wanted = lax.broadcasted_iota(jnp.int32, (2 * RIM, LANES), 0)
    wanted = jnp.where(wanted < RIM, wanted, wanted + FACES_PART - RIM)
    chosen = [
        jnp.where(wanted == names_ref[j : j + 1, :], 1.0, 0.0).astype(BF16)
        for j in range(4)
    ]
    lists = whole_pick(face_major(terms_ref), jnp.concatenate(chosen, 1))
    return lists[:FD, :RIM], lists[:FD, RIM:]


def first_kernel(
    padding_ref, inverse_hbm, coupling_hbm, interior_load_hbm, trace_load_hbm, shift_hbm, names_hbm,
    living_ref, own_ref, on_ref, off_ref, solved_hbm,
    solved_ref, inverse_ref, coupling_ref, interior_load_ref, trace_load_ref, shift_ref, names_ref, stage_ref, sems,
):
    rows = NI // PARTS
    copies = [pltpu.make_async_copy(interior_load_hbm, interior_load_ref, sems.at[0])]
    for part in range(PARTS):
        block = pl.ds(part * rows, rows)
        copies.append(
            pltpu.make_async_copy(inverse_hbm.at[block], inverse_ref.at[block], sems.at[1 + part])
        )
    rest = [
        (coupling_hbm, coupling_ref), (names_hbm, names_ref),
        (trace_load_hbm, trace_load_ref), (shift_hbm, shift_ref),
    ]
    for place, (source, target) in enumerate(rest):
        copies.append(pltpu.make_async_copy(source, target, sems.at[1 + PARTS + place]))
    for copy in [copies[0], copies[1 + PARTS], *copies[2 + PARTS :], *copies[1 : 1 + PARTS]]:
        copy.start()
    dom, sub = ids()
    for copy in copies[2 + PARTS :]:
        copy.wait()
    living = lane_iota(1) < LANES - padding_ref[0]
    living_ref[...] = jnp.broadcast_to(jnp.where(living, 1.0, 0.0), (8, LANES))
    stage_ref[NAMES:, :] = jnp.zeros((stage_ref.shape[0] - NAMES, LANES), F32)
    loads, load_exponent = coded(trace_load_ref[...])
    shifts, shift_exponent = coded(shift_ref[...])
    for half in range(2):
        columns = slice(half * RIM, half * RIM + RIM)
        first = FACES + 2 * FD * half
        stage_ref[first : first + FD, :] = loads[:, columns]
        stage_ref[first + FD : first + 2 * FD, :] = shifts[:, columns]
    stage_ref[NAMES : NAMES + 4, :] = names_ref[...].astype(F32)
    stage_ref[SCALES + 1 : SCALES + 2, :] = spread_row(load_exponent)
    stage_ref[SCALES + 2 : SCALES + 3, :] = spread_row(shift_exponent)
    copies[0].wait()
    load = interior_load_ref[...].astype(F32)
    solved = []
    for part in range(PARTS):
        copies[1 + part].wait()
        solved.append(matrix_times(inverse_ref.at[pl.ds(part * rows, rows)], load))
    solved = jnp.concatenate(solved, 0)
    solved_ref[...] = solved
    keep = pltpu.make_async_copy(solved_ref, solved_hbm, sems.at[PARTS + 5])
    keep.start()
    copies[1 + PARTS].wait()
    whole, exponent = coded(jnp.where(living, transposed_times(coupling_ref, solved), 0.0))
    stage_ref[:NF, :] = whole
    stage_ref[SCALES : SCALES + 1, :] = spread_row(exponent)
    low, high = rim_lists(stage_ref, names_ref)
    owner = sub == SUB - 1
    up = with_exponent(
        high * jnp.exp2(exponent - 15.0) + jnp.where(owner, trace_load_ref[:, RIM:], 0.0)
    )
    up += [jnp.where(owner, shifts[:, RIM:], 0.0), spread_row(shift_exponent)]
    down = [low, spread_row(exponent), jnp.zeros((FD + 1, LANES), F32)]
    put_lists(on_ref, off_ref, up, down, dom)
    own_ref[...] = as_sent(stage_ref[...])
    keep.wait()


def spread_rows(values, block):
    a = jnp.broadcast_to(values[2 * block : 2 * block + 1], (8, LANES))
    b = jnp.broadcast_to(values[2 * block + 1 : 2 * block + 2], (8, LANES))
    return jnp.where(row_iota(8) < 4, a, b)


def turn(values, steps):
    if steps == 0:
        return values
    rows = row_iota(8) & 3
    return jnp.where(
        rows < 4 - steps, pltpu.roll(values, 8 - steps, 0), pltpu.roll(values, 4 - steps, 0)
    )


def take_lanes(values, lanes):
    return jnp.take_along_axis(values, lanes, axis=1, mode="promise_in_bounds")


def partner_terms(gathered_ref, chunk, lane, low_list, high_list):
    rows = row_iota(8) & 3
    found = [jnp.zeros((8, LANES), F32) for _ in range(6)]
    for t in range(4):
        chunk_t = turn(chunk, (4 - t) % 4)
        lane_t = turn(lane, (4 - t) % 4)
        part = [jnp.zeros((8, LANES), F32) for _ in range(6)]
        for s in range(SUB):
            here = chunk_t == 4 * s + rows
            for g in range(6):
                taken = take_lanes(gathered_ref[s, 8 * g : 8 * g + 8, :], lane_t)
                part[g] = jnp.where(here, taken, part[g])
        for g in range(6):
            found[g] = found[g] + turn(part[g], t)
    on_low = chunk == 4 * SUB
    on_high = chunk == 4 * SUB + 1
    for g in range(6):
        found[g] = jnp.where(on_low, take_lanes(spread_rows(low_list, g), lane), found[g])
        found[g] = jnp.where(on_high, take_lanes(spread_rows(high_list, g), lane), found[g])
    return jnp.concatenate(found, 0)


def twice(slots):
    return jnp.concatenate([slots, slots], 0)


def six_times(rows8):
    return jnp.concatenate([rows8] * 6, 0)


def summed(gathered_ref, first, last):
    total = gathered_ref[0, first:last, :]
    for s in range(1, SUB):
        total = total + gathered_ref[s, first:last, :]
    return total


def partner_places(names_ref, gathered_ref, sub):
    weights, columns = [], []
    high_rows = row_iota(24)
    low_rows = row_iota(LANES)
    for s in range(SUB):
        for j in range(4):
            names = gathered_ref[s, NAMES + j : NAMES + j + 1, :].astype(jnp.int32)
            row_hit = (names >> 7) == high_rows
            weights.append(
                jnp.concatenate(
                    [
                        jnp.where(row_hit, F32(4 * s + j), 0.0),
                        jnp.where(row_hit, lane_iota(24).astype(F32), 0.0),
                    ],
                    0,
                ).astype(BF16)
            )
            columns.append(jnp.where((names & 127) == low_rows, 1.0, 0.0).astype(BF16))
    table = lax.dot_general(
        jnp.concatenate(weights, 1),
        jnp.concatenate(columns, 1),
        (((1,), (1,)), ((), ())),
        preferred_element_type=F32,
    )
    chunks, lanes = [], []
    for j in range(4):
        name = names_ref[j : j + 1, :]
        low = jnp.broadcast_to(name & 127, (24, LANES))
        hit = high_rows == (name >> 7)
        chunk_sum = jnp.where(hit, take_lanes(table[:24], low), 0.0).sum(0, keepdims=True)
        lane_sum = jnp.where(hit, take_lanes(table[24:], low), 0.0).sum(0, keepdims=True)
        chunk = chunk_sum.astype(jnp.int32) - (4 * sub + j)
        lane = lane_sum.astype(jnp.int32) - lane_iota(1)
        below, above = name < RIM, name >= FACES_PART
        chunk = jnp.where(below, 4 * SUB, jnp.where(above, 4 * SUB + 1, chunk))
        lane = jnp.where(below | above, name & 127, lane)
        chunks.append(chunk)
        lanes.append(lane)
    return jnp.concatenate(chunks, 0), jnp.concatenate(lanes, 0) & 127


def face_values(names_ref, gathered_ref, up_list, loads_ref, shifts_ref):
    for j in range(4):
        name = names_ref[j : j + 1, :]
        high = jnp.broadcast_to(name >> 7, (24, LANES))
        low = jnp.broadcast_to(name & 127, (24, LANES))
        got = jnp.where(high == 0, take_lanes(up_list, low), 0.0)
        for s in range(SUB):
            for half in range(2):
                first = FACES + 2 * FD * half
                source = gathered_ref[s, first : first + 2 * FD, :]
                got = jnp.where(high == 2 * s + half + 1, take_lanes(source, low), got)
        loads_ref[pl.ds(j, FD, stride=4), :] = got[:FD]
        shifts_ref[pl.ds(j, FD, stride=4), :] = got[FD:]


def put_terms(terms, base, names_ref, own_ref, on_ref, off_ref, stage_ref, dom):
    whole, exponent = coded(terms)
    exponent = exponent + base
    stage_ref[:NF, :] = whole
    stage_ref[NF:, :] = jnp.broadcast_to(exponent + BIAS, (stage_ref.shape[0] - NF, LANES))
    own_ref[...] = as_sent(stage_ref[...])
    low, high = rim_lists(stage_ref, names_ref)
    put_lists(on_ref, off_ref, [high, spread_row(exponent)], [low, spread_row(exponent)], dom)


def second_kernel(
    inverse_ref, coupling_ref, trace_ref, names_ref, living_ref, sent_ref,
    chunk_ref, lane_ref, valid_ref, weight_ref, shifts_ref, view_ref, terms_ref, inner_ref, scale_ref, own_ref, on_ref, off_ref,
    loads_ref, stage_ref, gathered_ref,
):
    dom, sub = ids()
    count = lax.axis_size("dom")
    base = decode_first(sent_ref, gathered_ref)
    scale_ref[...] = jnp.broadcast_to(base, (8, LANES))
    chunk, lane = partner_places(names_ref, gathered_ref, sub)
    chunk, lane = twice(chunk), twice(lane)
    names = twice(names_ref[...])
    valid = jnp.where((names < RIM) & (dom == 0), 0.0, 1.0)
    weight = jnp.where((names >= FACES_PART) & (dom == count - 1), 1.0, 0.5)
    chunk_ref[...] = chunk
    lane_ref[...] = lane
    valid_ref[...] = valid
    weight_ref[...] = weight
    up_list = jnp.concatenate(
        [summed(gathered_ref, UP, UP + FD), summed(gathered_ref, UP_SHIFT, UP_SHIFT + FD)], 0
    )
    down_list = summed(gathered_ref, DOWN, DOWN + FD)
    face_values(names_ref, gathered_ref, up_list, loads_ref, shifts_ref)
    own_load = jnp.where(six_times(names) < RIM, 0.0, loads_ref[...])
    partner = partner_terms(gathered_ref, chunk, lane, up_list[:FD], down_list)
    view = jnp.where(six_times(valid) > 0.0, own_load + (gathered_ref[sub, :NF, :] + partner), 0.0)
    view_ref[...] = view
    def keep(inner):
        inner_ref[...] = inner

    terms = element_operator(inverse_ref, coupling_ref, trace_ref, view, living_ref, keep)
    terms_ref[...] = terms
    put_terms(terms, base, names_ref, own_ref, on_ref, off_ref, stage_ref, dom)


def next_view(factor, gathered_ref, chunk_ref, lane_ref, valid_ref, shifts_ref, view_ref, terms_ref):
    low_list = summed(gathered_ref, LATER_UP, LATER_UP + FD)
    high_list = summed(gathered_ref, LATER_DOWN, LATER_DOWN + FD)
    partner = partner_terms(gathered_ref, chunk_ref[...], lane_ref[...], low_list, high_list)
    image = factor * (terms_ref[...] + shifts_ref[...] * view_ref[...]) + partner
    return jnp.where(six_times(valid_ref[...]) > 0.0, image, 0.0)


def third_kernel(
    inverse_ref, coupling_ref, trace_ref, names_ref, living_ref, sent_ref,
    chunk_ref, lane_ref, valid_ref, shifts_ref, view_ref, terms_ref, scale_ref, before_ref,
    new_view_ref, new_terms_ref, inner_ref, new_scale_ref, own_ref, on_ref, off_ref,
    stage_ref, gathered_ref,
):
    dom, _ = ids()
    scale = scale_ref[:1, :]
    base = decode_later(sent_ref, gathered_ref, scale)
    new_scale_ref[...] = jnp.where(row_iota(8) == 0, scale, base)
    factor = jnp.exp2(scale - base)
    view = next_view(factor, gathered_ref, chunk_ref, lane_ref, valid_ref, shifts_ref, view_ref, terms_ref)
    new_view_ref[...] = view
    inner_ref[0] = before_ref[...]

    def keep(inner):
        inner_ref[1] = inner

    terms = element_operator(inverse_ref, coupling_ref, trace_ref, view, living_ref, keep)
    new_terms_ref[...] = terms
    put_terms(terms, base, names_ref, own_ref, on_ref, off_ref, stage_ref, dom)


def fourth_kernel(
    inverse_ref, coupling_ref, trace_ref, living_ref, sent_ref,
    chunk_ref, lane_ref, valid_ref, weight_ref, shifts_ref, first_view_ref, view_ref, terms_ref, scale_ref, before_ref,
    inner_hbm, sums_hbm,
    inner_ref, sums_ref, gathered_ref, sems,
):
    copies = [
        pltpu.make_async_copy(before_ref, inner_hbm.at[pl.ds(0, 2)], sems.at[0]),
        pltpu.make_async_copy(inner_ref, inner_hbm.at[2], sems.at[1]),
    ]
    copies[0].start()

    def keep(inner):
        inner_ref[...] = inner
        copies[1].start()

    scales = [scale_ref[:1, :], scale_ref[1:2, :]]
    scales.append(decode_later(sent_ref, gathered_ref, scales[1]))
    factor = jnp.exp2(scales[1] - scales[2])
    first, second = first_view_ref[...], view_ref[...]
    third = next_view(factor, gathered_ref, chunk_ref, lane_ref, valid_ref, shifts_ref, view_ref, terms_ref)
    last = element_operator(inverse_ref, coupling_ref, trace_ref, third, living_ref, keep)
    weight = six_times(weight_ref[...])
    last = last + weight * (shifts_ref[...] * third)
    views = (first, second, third)
    weighted = [weight * view for view in views]
    products = [weighted[i] * views[j] for i in range(3) for j in range(i, 3)]
    products += [view * last for view in views]
    powers = [scales[i] + scales[j] for i in range(3) for j in range(i, 3)]
    powers += [scale + scales[2] for scale in scales]
    lane = lane_iota(1)
    sums = jnp.zeros((1, LANES), F32)
    for place, product in enumerate(products):
        sums = sums + jnp.where(lane == SCALE_LANE + place, powers[place], 0.0)
        total = product.reshape(6, 8, LANES).sum(0).sum(0, keepdims=True).sum(1, keepdims=True)
        sums = sums + jnp.where(lane == place, total, 0.0)
    sums_ref[...] = jnp.broadcast_to(sums, sums_ref.shape)
    send = pltpu.make_async_copy(sums_ref, sums_hbm, sems.at[2])
    send.start()
    for copy in copies:
        copy.wait()
    send.wait()


def owner_kernel(
    first_sent_ref, second_sent_ref, third_sent_ref, trace_load_hbm, shift_hbm, *rest,
):
    solved_hbm, inner_hbm = rest[:2]
    owned_ref, kept_ref, terms_ref, chosen_ref, first_ref, second_ref, third_ref = rest[2:9]
    trace_load_ref, shift_ref, sems = rest[9:]
    copies = [
        pltpu.make_async_copy(trace_load_hbm, trace_load_ref, sems.at[0]),
        pltpu.make_async_copy(shift_hbm, shift_ref, sems.at[1]),
        pltpu.make_async_copy(solved_hbm, kept_ref.at[0], sems.at[2]),
        pltpu.make_async_copy(inner_hbm, kept_ref.at[pl.ds(1, 3)], sems.at[3]),
    ]
    for copy in copies:
        copy.start()
    scales = [decode_first(first_sent_ref, first_ref)]
    scales.append(decode_later(second_sent_ref, second_ref, scales[0]))
    scales.append(decode_later(third_sent_ref, third_ref, scales[1]))
    _, sub = ids()
    wanted = lax.broadcasted_iota(jnp.int32, (2 * RIM, LANES), 0) + (RIM + 2 * RIM * sub)
    sources = (first_ref, second_ref, third_ref)
    for s in range(SUB):
        for j in range(4):
            columns = slice((4 * s + j) * LANES, (4 * s + j + 1) * LANES)
            names = first_ref[s, NAMES + j : NAMES + j + 1, :].astype(jnp.int32)
            chosen_ref[:, columns] = jnp.where(wanted == names, 1.0, 0.0).astype(BF16)
            for v, source in enumerate(sources):
                part = source[s, pl.ds(j, FD, stride=4), :]
                part = jnp.concatenate([part, jnp.zeros((4, LANES), F32)], 0)
                for piece, value in enumerate(split3(part)):
                    first = 16 * (3 * v + piece)
                    terms_ref[first : first + 16, columns] = value
    sums = lax.dot_general(
        terms_ref[...], chosen_ref[...], (((1,), (1,)), ((), ())), preferred_element_type=F32
    )
    for copy in copies:
        copy.wait()
    last = sub == SUB - 1
    downs = (
        summed(first_ref, DOWN, DOWN + FD),
        summed(second_ref, LATER_DOWN, LATER_DOWN + FD),
        summed(third_ref, LATER_DOWN, LATER_DOWN + FD),
    )
    current = None
    for v in range(3):
        rows = [sums[48 * v + 16 * piece : 48 * v + 16 * piece + FD] for piece in range(3)]
        total = rows[0] + rows[1] + rows[2]
        down = jnp.concatenate(
            [jnp.zeros((FD, RIM), F32), jnp.where(last, downs[v], 0.0)], 1
        )
        total = total + down
        if v == 0:
            current = total + jnp.exp2(-scales[0][:, :1]) * trace_load_ref[...]
        else:
            factor = jnp.exp2(scales[v - 1] - scales[v])[:, :1]
            current = total + factor * (shift_ref[...] * current)
        owned_ref[v] = current


def coefficients(sums, powers, own_powers):
    lane = lane_iota(1)

    def entry(row, place):
        return jnp.where(lane == place, row, 0.0).sum(1, keepdims=True)

    pairs = [(i, j) for i in range(3) for j in range(i, 3)]
    pairs += [(i, 3) for i in range(3)]
    places = [pairs.index((i, i)) for i in range(3)]
    scales = [0.5 * entry(powers, place) for place in places]
    own_scales = [0.5 * entry(own_powers, place) for place in places]
    table = {}
    for place, (i, j) in enumerate(pairs):
        power = entry(powers, place) - scales[i] - scales[min(j, 2)]
        table[i, j] = table[j, i] = entry(sums, place) * jnp.exp2(power)
    steps = [jnp.exp2(scales[1] - scales[0]), jnp.exp2(scales[2] - scales[1]), 1.0]

    def form(left, right):
        total = None
        for i, a in enumerate(left):
            for j, b in enumerate(right):
                if a is None or b is None:
                    continue
                term = a * b * table[i, j]
                total = term if total is None else total + term
        return total

    def combine(left, factor, right):
        merged = []
        for i in range(max(len(left), len(right))):
            a = left[i] if i < len(left) else None
            b = right[i] if i < len(right) else None
            if b is None:
                merged.append(a)
            else:
                merged.append(factor * b if a is None else a + factor * b)
        return merged

    one = jnp.ones((1, 1), F32)
    residual, direction, result = [one], [one], []
    norm = table[0, 0]
    for iteration in range(3):
        image = [None] + [a * b for a, b in zip(direction, steps, strict=False)]
        step = norm / form(direction, image)
        result = combine(result, step, direction)
        if iteration < 2:
            residual = combine(residual, -step, image)
            new_norm = form(residual, residual)
            direction = combine(residual, new_norm / norm, direction)
            norm = new_norm
    return [
        part * jnp.exp2(scales[0] - scale + own)
        for part, scale, own in zip(result, scales, own_scales, strict=True)
    ]


def last_kernel(
    living_ref, all_sums_ref, inner_ref, owned_ref,
    traces_ref, interior_ref,
):
    dom, sub = ids()
    sums = all_sums_ref[...]
    powers = pltpu.roll(sums, LANES - SCALE_LANE, 1)
    own = pltpu.roll(all_sums_ref[pl.ds(dom * SUB + sub, 1), :], LANES - SCALE_LANE, 1)
    used = lane_iota(1) < SCALE_LANE
    powers, own = jnp.where(used, powers, 0.0), jnp.where(used, own, 0.0)
    top = powers.reshape(-1, 8, LANES).max(0).max(0, keepdims=True)
    sums = (sums * jnp.exp2(powers - top)).reshape(-1, 8, LANES).sum(0).sum(0, keepdims=True)
    a, b, c = coefficients(sums, top, own)
    traces_ref[...] = a * owned_ref[0] + b * owned_ref[1] + c * owned_ref[2]
    lifted = a * inner_ref[1] + b * inner_ref[2] + c * inner_ref[3]
    living = jnp.broadcast_to(living_ref[:1, :], (NI, LANES)) > 0.0
    interior_ref[...] = jnp.where(living, inner_ref[0] - lifted, 0.0)


def call(kernel, outputs, inputs, scratch=(), limit=6, from_hbm=(), to_hbm=()):
    held = [pltpu.with_memory_space_constraint(x, pltpu.HBM) for x in from_hbm]
    near, far = pl.BlockSpec(memory_space=pltpu.VMEM), pl.BlockSpec(memory_space=pltpu.HBM)
    return pl.pallas_call(
        kernel,
        out_shape=[jax.ShapeDtypeStruct(s, d) for s, d in outputs]
        + [pltpu.HBM(s, d) for s, d in to_hbm],
        in_specs=[near if x.ndim > 1 else pl.BlockSpec(memory_space=pltpu.SMEM) for x in inputs]
        + [far] * len(held),
        out_specs=[near] * len(outputs) + [far] * len(to_hbm),
        scratch_shapes=list(scratch),
        compiler_params=pltpu.CompilerParams(vmem_limit_bytes=limit * MIB),
    )(*inputs, *held)


def to_all(blocks):
    value = jnp.concatenate(blocks, 0)
    copies = jnp.broadcast_to(value[None], (SUB,) + value.shape)
    return lax.all_to_all(copies, "sub", 0, 0, tiled=True)


def neighbours(on, off):
    count = lax.axis_size("dom")
    pairs = [(i, i + 1) for i in range(1, count - 1, 2)]
    from_off = lax.ppermute(off, "dom", pairs + [(j, i) for i, j in pairs])
    from_on = lax.ppermute(on, "dom", [(i, i ^ 1) for i in range(count)])
    even = lax.axis_index("dom") % 2 == 0
    return jnp.where(even, from_off, from_on), jnp.where(even, from_on, from_off)


def later(own, on, off):
    from_below, from_above = neighbours(on, off)
    return to_all([own[:LATER_UP], from_below[: FD + 1], from_above[: FD + 1]])


def on_device(
    interior_inverse, coupling, trace_block, interior_load, trace_load, face_shift, element_faces, block_padding,
):
    slab, rows8 = ((NF, LANES), F32), ((8, LANES), F32)
    places = ((8, LANES), jnp.int32)
    sent = [((64, LANES), I16), ((16, LANES), I16), ((16, LANES), I16)]
    stage = pltpu.VMEM((64, LANES), F32)
    decoded = pltpu.VMEM((SUB, LATER_ROWS, LANES), F32)
    decoded_first = pltpu.VMEM((SUB, FIRST_ROWS, LANES), F32)
    matrices = [interior_inverse, coupling, trace_block]

    inner = ((NI, LANES), F32)

    living, own, on, off, solved = call(
        first_kernel,
        [rows8, ((112, LANES), I16), ((32, LANES), I16), ((32, LANES), I16)],
        [block_padding],
        from_hbm=[interior_inverse, coupling, interior_load, trace_load, face_shift, element_faces],
        to_hbm=[inner],
        scratch=[
            pltpu.VMEM((NI, LANES), F32), pltpu.VMEM((NI, NI, LANES), BF16), pltpu.VMEM((NI, NF, LANES), BF16),
            pltpu.VMEM((NI, LANES), BF16), pltpu.VMEM((FD, 2 * RIM), F32), pltpu.VMEM((FD, 2 * RIM), F32),
            pltpu.VMEM((4, LANES), jnp.int32), pltpu.VMEM((112, LANES), F32),
            pltpu.SemaphoreType.DMA((PARTS + 6,)),
        ],
        limit=10,
    )
    *matrices, own = lax.optimization_barrier((*matrices, own))
    from_below, from_above = neighbours(on, off)
    first = to_all([own[:UP], from_below[: DOWN - UP], from_above[: FIRST_ROWS - DOWN]])
    chunk, lane, valid, weight, shifts, view0, terms, kept, scale, own, on, off = call(
        second_kernel,
        [places, places, rows8, rows8, slab, slab, slab, inner, rows8, *sent],
        [*matrices, element_faces, living, first],
        scratch=[pltpu.VMEM((NF, LANES), F32), stage, decoded_first],
    )
    second = later(own, on, off)
    view1, terms1, kept, scale, own, on, off = call(
        third_kernel,
        [slab, slab, ((2, NI, LANES), F32), rows8, *sent],
        [*matrices, element_faces, living, second, chunk, lane, valid, shifts, view0, terms, scale, kept],
        scratch=[stage, decoded],
    )
    third = later(own, on, off)
    everyone = lax.axis_size("dom") * SUB
    kept, sums = call(
        fourth_kernel,
        [],
        [*matrices, living, third, chunk, lane, valid, weight, shifts, view0, view1, terms1, scale, kept],
        to_hbm=[((3, NI, LANES), F32), ((everyone, LANES), F32)],
        scratch=[
            pltpu.VMEM((NI, LANES), F32), pltpu.VMEM((everyone, LANES), F32), decoded,
            pltpu.SemaphoreType.DMA((3,)),
        ],
    )
    all_sums = lax.all_to_all(sums, ("dom", "sub"), 0, 0, tiled=True)
    owned, kept = call(
        owner_kernel,
        [((3, FD, 2 * RIM), F32), ((4, NI, LANES), F32)],
        [first, second, third],
        from_hbm=[trace_load, face_shift, solved, kept],
        scratch=[
            pltpu.VMEM((144, 32 * LANES), BF16), pltpu.VMEM((2 * RIM, 32 * LANES), BF16),
            decoded_first, decoded, decoded,
            pltpu.VMEM((FD, 2 * RIM), F32), pltpu.VMEM((FD, 2 * RIM), F32), pltpu.SemaphoreType.DMA((4,)),
        ],
        limit=14,
    )
    traces, interior = call(
        last_kernel,
        [((FD, 2 * RIM), F32), ((NI, LANES), F32)],
        [living, all_sums, kept, owned],
    )
    return traces, interior


def solution(mesh):
    last = ("dom", "sub")
    placed = (
        P(None, None, last), P(None, None, last), P(None, None, last),
        P(None, last), P(None, last), P(None, last), P(None, last), P(last),
    )
    return jax.shard_map(
        on_device,
        mesh=mesh,
        in_specs=placed,
        out_specs=(P(None, last), P(None, last)),
        check_vma=False,
    )
```

```python
import functools

import jax
import jax.numpy as jnp
from jax import lax
from jax.experimental import pallas as pl
from jax.experimental.pallas import tpu as pltpu
from jax.sharding import PartitionSpec as P

NI = 80
FD = 12
NF = 48
LANES = 128
RIM = 128
SUB = 8
FACES_PART = 2048
F32 = jnp.float32
BF16 = jnp.bfloat16
MIB = 1024 * 1024
PARTS = 5

I16 = jnp.int16

BIAS = 16384.0
SCALE_LANE = 64
MATE_LANE = 16
FACES, NAMES, SCALES, UP, UP_SHIFT, DOWN, FIRST_ROWS = 48, 96, 100, 105, 118, 131, 144
LATER_UP, LATER_DOWN, LATER_ROWS = 54, 67, 80


def row_iota(rows):
    return lax.broadcasted_iota(jnp.int32, (rows, LANES), 0)


def lane_iota(rows):
    return lax.broadcasted_iota(jnp.int32, (rows, LANES), 1)


def eight_sums(parts):
    rows = row_iota(8)
    low = rows < 4
    parts = [
        jnp.where(low, parts[i], parts[i + 4])
        + pltpu.roll(jnp.where(low, parts[i + 4], parts[i]), 4, 0)
        for i in range(4)
    ]
    for step in (2, 1):
        low = (rows & step) == 0
        parts = [
            jnp.where(
                low,
                parts[i] + pltpu.roll(parts[i], 8 - step, 0),
                parts[i + step] + pltpu.roll(parts[i + step], step, 0),
            )
            for i in range(step)
        ]
    return parts[0]


def matrix_times(matrix_ref, vector):
    rows, depth, _ = matrix_ref.shape
    blocks = []
    for first in range(0, rows, 8):
        parts = [
            (matrix_ref[first + i].astype(F32) * vector)
            .reshape(depth // 8, 8, LANES)
            .sum(0)
            for i in range(8)
        ]
        blocks.append(eight_sums(parts))
    return jnp.concatenate(blocks, 0)


def transposed_times(matrix_ref, vector):
    depth = matrix_ref.shape[0]
    totals = [None, None]
    for i in range(depth):
        term = matrix_ref[i].astype(F32) * vector[i : i + 1]
        totals[i % 2] = term if totals[i % 2] is None else totals[i % 2] + term
    return totals[0] + totals[1]


def coded(value):
    top = jnp.abs(value).max(0, keepdims=True).max(1, keepdims=True)
    exponent = jnp.floor(jnp.log2(jnp.maximum(top, 2.0**-100))) + 1.0
    whole = jnp.floor(value * jnp.exp2(15.0 - exponent) + 0.5)
    return jnp.clip(whole, -32767.0, 32767.0), exponent


def spread_row(exponent):
    return jnp.broadcast_to(exponent + BIAS, (1, LANES))


def as_sent(value):
    return value.astype(jnp.int32).astype(I16)


def with_exponent(value):
    whole, exponent = coded(value)
    return [whole, spread_row(exponent)]


def put_lists(on_ref, off_ref, up, down, dom):
    even = dom % 2 == 0
    rest = [jnp.zeros((on_ref.shape[0] - sum(len(x) for x in up), LANES), F32)]
    up, down = jnp.concatenate(up + rest, 0), jnp.concatenate(down + rest, 0)
    on_ref[...] = as_sent(jnp.where(even, up, down))
    off_ref[...] = as_sent(jnp.where(even, down, up))


def decode(sent_ref, terms_ref, sections, scale_rows, least=None):
    rows = sent_ref.shape[1]
    row = row_iota(rows)
    for s in range(SUB):
        terms_ref[s] = sent_ref[s].astype(jnp.int32).astype(F32)
    base = least
    for s in range(SUB):
        for place in scale_rows:
            exponent = terms_ref[s, place : place + 1, :] - BIAS
            base = exponent if base is None else jnp.maximum(base, exponent)
    for s in range(SUB):
        factors = jnp.ones((1, LANES), F32)
        for end, exponent, scaled in reversed(sections):
            if exponent is None:
                factor = jnp.ones((1, LANES), F32)
            else:
                power = terms_ref[s, exponent : exponent + 1, :] - (BIAS + 15.0)
                factor = jnp.exp2(power - base if scaled else power)
            factors = jnp.where(row < end, factor, factors)
        terms_ref[s] = terms_ref[s] * factors
    return base


def decode_first(sent_ref, terms_ref):
    return decode(
        sent_ref,
        terms_ref,
        [
            (FACES, SCALES, True), (FACES + FD, SCALES + 1, True), (FACES + 2 * FD, SCALES + 2, False),
            (FACES + 3 * FD, SCALES + 1, True), (NAMES, SCALES + 2, False), (UP, None, False),
            (UP + FD, UP + FD, True), (UP_SHIFT, None, False), (UP_SHIFT + FD, UP_SHIFT + FD, False),
            (DOWN, None, False), (FIRST_ROWS, DOWN + FD, True),
        ],
        (SCALES, SCALES + 1, UP + FD, DOWN + FD),
    )


def decode_later(sent_ref, terms_ref, before):
    return decode(
        sent_ref,
        terms_ref,
        [
            (NF, NF, True), (LATER_UP, None, False), (LATER_UP + FD, LATER_UP + FD, True),
            (LATER_DOWN, None, False), (LATER_ROWS, LATER_DOWN + FD, True),
        ],
        (NF, LATER_UP + FD, LATER_DOWN + FD),
        before + 3.0,
    )


def ids():
    return lax.axis_index("dom"), lax.axis_index("sub")


def element_operator(inverse_ref, coupling_ref, trace_ref, view, living_ref, keep):
    inner = matrix_times(inverse_ref, matrix_times(coupling_ref, view))
    keep(inner)
    terms = transposed_times(coupling_ref, inner) + matrix_times(trace_ref, view)
    return jnp.where(six_times(living_ref[...]) > 0.0, terms, 0.0)


def split3(value):
    high = value.astype(BF16)
    rest = value - high.astype(F32)
    middle = rest.astype(BF16)
    low = (rest - middle.astype(F32)).astype(BF16)
    return high, middle, low


def whole_pick(values, chosen):
    high = jnp.floor(values * (1.0 / 256.0))
    stacked = jnp.concatenate([high, values - 256.0 * high], 0).astype(BF16)
    sums = lax.dot_general(
        stacked, chosen, (((1,), (1,)), ((), ())), preferred_element_type=F32
    )
    rows = values.shape[0]
    return 256.0 * sums[:rows] + sums[rows:]


def face_major(terms_ref):
    slots = []
    for j in range(4):
        part = terms_ref[pl.ds(j, FD, stride=4), :]
        slots.append(jnp.concatenate([part, jnp.zeros((4, LANES), F32)], 0))
    return jnp.concatenate(slots, 1)


def rim_lists(terms_ref, names_ref):
    wanted = lax.broadcasted_iota(jnp.int32, (2 * RIM, LANES), 0)
    wanted = jnp.where(wanted < RIM, wanted, wanted + FACES_PART - RIM)
    chosen = [
        jnp.where(wanted == names_ref[j : j + 1, :], 1.0, 0.0).astype(BF16)
        for j in range(4)
    ]
    lists = whole_pick(face_major(terms_ref), jnp.concatenate(chosen, 1))
    return lists[:FD, :RIM], lists[:FD, RIM:]


def first_kernel(
    padding_ref, inverse_hbm, coupling_hbm, interior_load_hbm, trace_load_hbm, shift_hbm, names_hbm,
    living_ref, own_ref, on_ref, off_ref, solved_hbm,
    solved_ref, inverse_ref, coupling_ref, interior_load_ref, trace_load_ref, shift_ref, names_ref, stage_ref, sems,
):
    rows = NI // PARTS
    copies = [pltpu.make_async_copy(interior_load_hbm, interior_load_ref, sems.at[0])]
    for part in range(PARTS):
        block = pl.ds(part * rows, rows)
        copies.append(
            pltpu.make_async_copy(inverse_hbm.at[block], inverse_ref.at[block], sems.at[1 + part])
        )
    rest = [
        (coupling_hbm, coupling_ref), (names_hbm, names_ref),
        (trace_load_hbm, trace_load_ref), (shift_hbm, shift_ref),
    ]
    for place, (source, target) in enumerate(rest):
        copies.append(pltpu.make_async_copy(source, target, sems.at[1 + PARTS + place]))
    for copy in [copies[0], copies[1 + PARTS], *copies[2 + PARTS :], *copies[1 : 1 + PARTS]]:
        copy.start()
    dom, sub = ids()
    for copy in copies[2 + PARTS :]:
        copy.wait()
    living = lane_iota(1) < LANES - padding_ref[0]
    living_ref[...] = jnp.broadcast_to(jnp.where(living, 1.0, 0.0), (8, LANES))
    stage_ref[NAMES:, :] = jnp.zeros((stage_ref.shape[0] - NAMES, LANES), F32)
    loads, load_exponent = coded(trace_load_ref[...])
    shifts, shift_exponent = coded(shift_ref[...])
    for half in range(2):
        columns = slice(half * RIM, half * RIM + RIM)
        first = FACES + 2 * FD * half
        stage_ref[first : first + FD, :] = loads[:, columns]
        stage_ref[first + FD : first + 2 * FD, :] = shifts[:, columns]
    stage_ref[NAMES : NAMES + 4, :] = names_ref[...].astype(F32)
    stage_ref[SCALES + 1 : SCALES + 2, :] = spread_row(load_exponent)
    stage_ref[SCALES + 2 : SCALES + 3, :] = spread_row(shift_exponent)
    copies[0].wait()
    load = interior_load_ref[...].astype(F32)
    solved = []
    for part in range(PARTS):
        copies[1 + part].wait()
        solved.append(matrix_times(inverse_ref.at[pl.ds(part * rows, rows)], load))
    solved = jnp.concatenate(solved, 0)
    solved_ref[...] = solved
    keep = pltpu.make_async_copy(solved_ref, solved_hbm, sems.at[PARTS + 5])
    keep.start()
    copies[1 + PARTS].wait()
    whole, exponent = coded(jnp.where(living, transposed_times(coupling_ref, solved), 0.0))
    stage_ref[:NF, :] = whole
    stage_ref[SCALES : SCALES + 1, :] = spread_row(exponent)
    low, high = rim_lists(stage_ref, names_ref)
    owner = sub == SUB - 1
    up = with_exponent(
        high * jnp.exp2(exponent - 15.0) + jnp.where(owner, trace_load_ref[:, RIM:], 0.0)
    )
    up += [jnp.where(owner, shifts[:, RIM:], 0.0), spread_row(shift_exponent)]
    down = [low, spread_row(exponent), jnp.zeros((FD + 1, LANES), F32)]
    put_lists(on_ref, off_ref, up, down, dom)
    own_ref[...] = as_sent(stage_ref[...])
    keep.wait()


def spread_rows(values, block):
    a = jnp.broadcast_to(values[2 * block : 2 * block + 1], (8, LANES))
    b = jnp.broadcast_to(values[2 * block + 1 : 2 * block + 2], (8, LANES))
    return jnp.where(row_iota(8) < 4, a, b)


def turn(values, steps):
    if steps == 0:
        return values
    rows = row_iota(8) & 3
    return jnp.where(
        rows < 4 - steps, pltpu.roll(values, 8 - steps, 0), pltpu.roll(values, 4 - steps, 0)
    )


def take_lanes(values, lanes):
    return jnp.take_along_axis(values, lanes, axis=1, mode="promise_in_bounds")


def partner_terms(gathered_ref, chunk, lane, low_list, high_list):
    rows = row_iota(8) & 3
    found = [jnp.zeros((8, LANES), F32) for _ in range(6)]
    for t in range(4):
        chunk_t = turn(chunk, (4 - t) % 4)
        lane_t = turn(lane, (4 - t) % 4)
        part = [jnp.zeros((8, LANES), F32) for _ in range(6)]
        for s in range(SUB):
            here = chunk_t == 4 * s + rows
            for g in range(6):
                taken = take_lanes(gathered_ref[s, 8 * g : 8 * g + 8, :], lane_t)
                part[g] = jnp.where(here, taken, part[g])
        for g in range(6):
            found[g] = found[g] + turn(part[g], t)
    on_low = chunk == 4 * SUB
    on_high = chunk == 4 * SUB + 1
    for g in range(6):
        found[g] = jnp.where(on_low, take_lanes(spread_rows(low_list, g), lane), found[g])
        found[g] = jnp.where(on_high, take_lanes(spread_rows(high_list, g), lane), found[g])
    return jnp.concatenate(found, 0)


def twice(slots):
    return jnp.concatenate([slots, slots], 0)


def six_times(rows8):
    return jnp.concatenate([rows8] * 6, 0)


def summed(gathered_ref, first, last):
    total = gathered_ref[0, first:last, :]
    for s in range(1, SUB):
        total = total + gathered_ref[s, first:last, :]
    return total


def partner_places(names_ref, gathered_ref, sub):
    weights, columns = [], []
    high_rows = row_iota(24)
    low_rows = row_iota(LANES)
    for s in range(SUB):
        for j in range(4):
            names = gathered_ref[s, NAMES + j : NAMES + j + 1, :].astype(jnp.int32)
            row_hit = (names >> 7) == high_rows
            weights.append(
                jnp.concatenate(
                    [
                        jnp.where(row_hit, F32(4 * s + j), 0.0),
                        jnp.where(row_hit, lane_iota(24).astype(F32), 0.0),
                    ],
                    0,
                ).astype(BF16)
            )
            columns.append(jnp.where((names & 127) == low_rows, 1.0, 0.0).astype(BF16))
    table = lax.dot_general(
        jnp.concatenate(weights, 1),
        jnp.concatenate(columns, 1),
        (((1,), (1,)), ((), ())),
        preferred_element_type=F32,
    )
    chunks, lanes = [], []
    for j in range(4):
        name = names_ref[j : j + 1, :]
        low = jnp.broadcast_to(name & 127, (24, LANES))
        hit = high_rows == (name >> 7)
        chunk_sum = jnp.where(hit, take_lanes(table[:24], low), 0.0).sum(0, keepdims=True)
        lane_sum = jnp.where(hit, take_lanes(table[24:], low), 0.0).sum(0, keepdims=True)
        chunk = chunk_sum.astype(jnp.int32) - (4 * sub + j)
        lane = lane_sum.astype(jnp.int32) - lane_iota(1)
        below, above = name < RIM, name >= FACES_PART
        chunk = jnp.where(below, 4 * SUB, jnp.where(above, 4 * SUB + 1, chunk))
        lane = jnp.where(below | above, name & 127, lane)
        chunks.append(chunk)
        lanes.append(lane)
    return jnp.concatenate(chunks, 0), jnp.concatenate(lanes, 0) & 127


def face_values(names_ref, gathered_ref, up_list, loads_ref, shifts_ref):
    for j in range(4):
        name = names_ref[j : j + 1, :]
        high = jnp.broadcast_to(name >> 7, (24, LANES))
        low = jnp.broadcast_to(name & 127, (24, LANES))
        got = jnp.where(high == 0, take_lanes(up_list, low), 0.0)
        for s in range(SUB):
            for half in range(2):
                first = FACES + 2 * FD * half
                source = gathered_ref[s, first : first + 2 * FD, :]
                got = jnp.where(high == 2 * s + half + 1, take_lanes(source, low), got)
        loads_ref[pl.ds(j, FD, stride=4), :] = got[:FD]
        shifts_ref[pl.ds(j, FD, stride=4), :] = got[FD:]


def put_terms(terms, base, names_ref, own_ref, on_ref, off_ref, stage_ref, dom):
    whole, exponent = coded(terms)
    exponent = exponent + base
    stage_ref[:NF, :] = whole
    stage_ref[NF:, :] = jnp.broadcast_to(exponent + BIAS, (stage_ref.shape[0] - NF, LANES))
    own_ref[...] = as_sent(stage_ref[...])
    low, high = rim_lists(stage_ref, names_ref)
    put_lists(on_ref, off_ref, [high, spread_row(exponent)], [low, spread_row(exponent)], dom)


def second_kernel(
    inverse_ref, coupling_ref, trace_ref, names_ref, living_ref, sent_ref,
    chunk_ref, lane_ref, valid_ref, weight_ref, shifts_ref, view_ref, terms_ref, inner_ref, scale_ref, own_ref, on_ref, off_ref,
    loads_ref, stage_ref, gathered_ref,
):
    dom, sub = ids()
    count = lax.axis_size("dom")
    base = decode_first(sent_ref, gathered_ref)
    scale_ref[...] = jnp.broadcast_to(base, (8, LANES))
    chunk, lane = partner_places(names_ref, gathered_ref, sub)
    chunk, lane = twice(chunk), twice(lane)
    names = twice(names_ref[...])
    valid = jnp.where((names < RIM) & (dom == 0), 0.0, 1.0)
    weight = jnp.where((names >= FACES_PART) & (dom == count - 1), 1.0, 0.5)
    chunk_ref[...] = chunk
    lane_ref[...] = lane
    valid_ref[...] = valid
    weight_ref[...] = weight
    up_list = jnp.concatenate(
        [summed(gathered_ref, UP, UP + FD), summed(gathered_ref, UP_SHIFT, UP_SHIFT + FD)], 0
    )
    down_list = summed(gathered_ref, DOWN, DOWN + FD)
    face_values(names_ref, gathered_ref, up_list, loads_ref, shifts_ref)
    own_load = jnp.where(six_times(names) < RIM, 0.0, loads_ref[...])
    partner = partner_terms(gathered_ref, chunk, lane, up_list[:FD], down_list)
    view = jnp.where(six_times(valid) > 0.0, own_load + (gathered_ref[sub, :NF, :] + partner), 0.0)
    view_ref[...] = view
    def keep(inner):
        inner_ref[...] = inner

    terms = element_operator(inverse_ref, coupling_ref, trace_ref, view, living_ref, keep)
    terms_ref[...] = terms
    put_terms(terms, base, names_ref, own_ref, on_ref, off_ref, stage_ref, dom)


def next_view(factor, gathered_ref, chunk_ref, lane_ref, valid_ref, shifts_ref, view_ref, terms_ref):
    low_list = summed(gathered_ref, LATER_UP, LATER_UP + FD)
    high_list = summed(gathered_ref, LATER_DOWN, LATER_DOWN + FD)
    partner = partner_terms(gathered_ref, chunk_ref[...], lane_ref[...], low_list, high_list)
    image = factor * (terms_ref[...] + shifts_ref[...] * view_ref[...]) + partner
    return jnp.where(six_times(valid_ref[...]) > 0.0, image, 0.0)


def third_kernel(
    inverse_ref, coupling_ref, trace_ref, names_ref, living_ref, sent_ref,
    chunk_ref, lane_ref, valid_ref, shifts_ref, view_ref, terms_ref, scale_ref, before_ref,
    new_view_ref, new_terms_ref, inner_ref, new_scale_ref, own_ref, on_ref, off_ref,
    stage_ref, gathered_ref,
):
    dom, _ = ids()
    scale = scale_ref[:1, :]
    base = decode_later(sent_ref, gathered_ref, scale)
    new_scale_ref[...] = jnp.where(row_iota(8) == 0, scale, base)
    factor = jnp.exp2(scale - base)
    view = next_view(factor, gathered_ref, chunk_ref, lane_ref, valid_ref, shifts_ref, view_ref, terms_ref)
    new_view_ref[...] = view
    inner_ref[0] = before_ref[...]

    def keep(inner):
        inner_ref[1] = inner

    terms = element_operator(inverse_ref, coupling_ref, trace_ref, view, living_ref, keep)
    new_terms_ref[...] = terms
    put_terms(terms, base, names_ref, own_ref, on_ref, off_ref, stage_ref, dom)


def fourth_kernel(
    inverse_ref, coupling_ref, trace_ref, living_ref, sent_ref,
    chunk_ref, lane_ref, valid_ref, weight_ref, shifts_ref, first_view_ref, view_ref, terms_ref, scale_ref, before_ref,
    sums_ref, for_mate_ref, inner_hbm,
    inner_ref, gathered_ref, sems,
):
    copies = [
        pltpu.make_async_copy(before_ref, inner_hbm.at[pl.ds(0, 2)], sems.at[0]),
        pltpu.make_async_copy(inner_ref, inner_hbm.at[2], sems.at[1]),
    ]
    copies[0].start()

    def keep(inner):
        inner_ref[...] = inner
        copies[1].start()

    scales = [scale_ref[:1, :], scale_ref[1:2, :]]
    scales.append(decode_later(sent_ref, gathered_ref, scales[1]))
    factor = jnp.exp2(scales[1] - scales[2])
    first, second = first_view_ref[...], view_ref[...]
    third = next_view(factor, gathered_ref, chunk_ref, lane_ref, valid_ref, shifts_ref, view_ref, terms_ref)
    last = element_operator(inverse_ref, coupling_ref, trace_ref, third, living_ref, keep)
    weight = six_times(weight_ref[...])
    last = last + weight * (shifts_ref[...] * third)
    views = (first, second, third)
    weighted = [weight * view for view in views]
    products = [weighted[i] * views[j] for i in range(3) for j in range(i, 3)]
    products += [view * last for view in views]
    powers = [scales[i] + scales[j] for i in range(3) for j in range(i, 3)]
    powers += [scale + scales[2] for scale in scales]
    lane = lane_iota(1)
    sums = jnp.zeros((1, LANES), F32)
    for place, product in enumerate(products):
        sums = sums + jnp.where(lane == SCALE_LANE + place, powers[place], 0.0)
        total = product.reshape(6, 8, LANES).sum(0).sum(0, keepdims=True).sum(1, keepdims=True)
        sums = sums + jnp.where(lane == place, total, 0.0)
    sums_ref[...] = sums
    for_mate_ref[...] = pltpu.roll(sums, MATE_LANE, 1)
    for copy in copies:
        copy.wait()


def owner_kernel(
    first_sent_ref, second_sent_ref, third_sent_ref, trace_load_hbm, shift_hbm, *rest,
):
    solved_hbm, inner_hbm = rest[:2]
    owned_ref, kept_ref, terms_ref, chosen_ref, first_ref, second_ref, third_ref = rest[2:9]
    trace_load_ref, shift_ref, sems = rest[9:]
    copies = [
        pltpu.make_async_copy(trace_load_hbm, trace_load_ref, sems.at[0]),
        pltpu.make_async_copy(shift_hbm, shift_ref, sems.at[1]),
        pltpu.make_async_copy(solved_hbm, kept_ref.at[0], sems.at[2]),
        pltpu.make_async_copy(inner_hbm, kept_ref.at[pl.ds(1, 3)], sems.at[3]),
    ]
    for copy in copies:
        copy.start()
    scales = [decode_first(first_sent_ref, first_ref)]
    scales.append(decode_later(second_sent_ref, second_ref, scales[0]))
    scales.append(decode_later(third_sent_ref, third_ref, scales[1]))
    _, sub = ids()
    wanted = lax.broadcasted_iota(jnp.int32, (2 * RIM, LANES), 0) + (RIM + 2 * RIM * sub)
    sources = (first_ref, second_ref, third_ref)
    for s in range(SUB):
        for j in range(4):
            columns = slice((4 * s + j) * LANES, (4 * s + j + 1) * LANES)
            names = first_ref[s, NAMES + j : NAMES + j + 1, :].astype(jnp.int32)
            chosen_ref[:, columns] = jnp.where(wanted == names, 1.0, 0.0).astype(BF16)
            for v, source in enumerate(sources):
                part = source[s, pl.ds(j, FD, stride=4), :]
                part = jnp.concatenate([part, jnp.zeros((4, LANES), F32)], 0)
                for piece, value in enumerate(split3(part)):
                    first = 16 * (3 * v + piece)
                    terms_ref[first : first + 16, columns] = value
    sums = lax.dot_general(
        terms_ref[...], chosen_ref[...], (((1,), (1,)), ((), ())), preferred_element_type=F32
    )
    for copy in copies:
        copy.wait()
    last = sub == SUB - 1
    downs = (
        summed(first_ref, DOWN, DOWN + FD),
        summed(second_ref, LATER_DOWN, LATER_DOWN + FD),
        summed(third_ref, LATER_DOWN, LATER_DOWN + FD),
    )
    current = None
    for v in range(3):
        rows = [sums[48 * v + 16 * piece : 48 * v + 16 * piece + FD] for piece in range(3)]
        total = rows[0] + rows[1] + rows[2]
        down = jnp.concatenate(
            [jnp.zeros((FD, RIM), F32), jnp.where(last, downs[v], 0.0)], 1
        )
        total = total + down
        if v == 0:
            current = total + jnp.exp2(-scales[0][:, :1]) * trace_load_ref[...]
        else:
            factor = jnp.exp2(scales[v - 1] - scales[v])[:, :1]
            current = total + factor * (shift_ref[...] * current)
        owned_ref[v] = current


def coefficients(sums, powers, own_powers):
    lane = lane_iota(1)

    def entry(row, place):
        return jnp.where(lane == place, row, 0.0).sum(1, keepdims=True)

    pairs = [(i, j) for i in range(3) for j in range(i, 3)]
    pairs += [(i, 3) for i in range(3)]
    places = [pairs.index((i, i)) for i in range(3)]
    scales = [0.5 * entry(powers, place) for place in places]
    own_scales = [0.5 * entry(own_powers, place) for place in places]
    table = {}
    for place, (i, j) in enumerate(pairs):
        power = entry(powers, place) - scales[i] - scales[min(j, 2)]
        table[i, j] = table[j, i] = entry(sums, place) * jnp.exp2(power)
    steps = [jnp.exp2(scales[1] - scales[0]), jnp.exp2(scales[2] - scales[1]), 1.0]

    def form(left, right):
        total = None
        for i, a in enumerate(left):
            for j, b in enumerate(right):
                if a is None or b is None:
                    continue
                term = a * b * table[i, j]
                total = term if total is None else total + term
        return total

    def combine(left, factor, right):
        merged = []
        for i in range(max(len(left), len(right))):
            a = left[i] if i < len(left) else None
            b = right[i] if i < len(right) else None
            if b is None:
                merged.append(a)
            else:
                merged.append(factor * b if a is None else a + factor * b)
        return merged

    one = jnp.ones((1, 1), F32)
    residual, direction, result = [one], [one], []
    norm = table[0, 0]
    for iteration in range(3):
        image = [None] + [a * b for a, b in zip(direction, steps, strict=False)]
        step = norm / form(direction, image)
        result = combine(result, step, direction)
        if iteration < 2:
            residual = combine(residual, -step, image)
            new_norm = form(residual, residual)
            direction = combine(residual, new_norm / norm, direction)
            norm = new_norm
    return [
        part * jnp.exp2(scales[0] - scale + own)
        for part, scale, own in zip(result, scales, own_scales, strict=True)
    ]


def last_kernel(
    living_ref, all_sums_ref, inner_ref, owned_ref,
    traces_ref, interior_ref,
):
    dom, sub = ids()
    sums = all_sums_ref[...]
    sums = jnp.concatenate([sums, pltpu.roll(sums, LANES - MATE_LANE, 1)], 0)
    powers = pltpu.roll(sums, LANES - SCALE_LANE, 1)
    own = pltpu.roll(all_sums_ref[pl.ds((dom // 2) * SUB + sub, 1), :], LANES - SCALE_LANE, 1)
    used = lane_iota(1) < MATE_LANE
    powers, own = jnp.where(used, powers, 0.0), jnp.where(used, own, 0.0)
    top = powers.reshape(-1, 8, LANES).max(0).max(0, keepdims=True)
    sums = (sums * jnp.exp2(powers - top)).reshape(-1, 8, LANES).sum(0).sum(0, keepdims=True)
    a, b, c = coefficients(sums, top, own)
    traces_ref[...] = a * owned_ref[0] + b * owned_ref[1] + c * owned_ref[2]
    lifted = a * inner_ref[1] + b * inner_ref[2] + c * inner_ref[3]
    living = jnp.broadcast_to(living_ref[:1, :], (NI, LANES)) > 0.0
    interior_ref[...] = jnp.where(living, inner_ref[0] - lifted, 0.0)


def call(kernel, outputs, inputs, scratch=(), limit=6, from_hbm=(), to_hbm=()):
    held = [pltpu.with_memory_space_constraint(x, pltpu.HBM) for x in from_hbm]
    near, far = pl.BlockSpec(memory_space=pltpu.VMEM), pl.BlockSpec(memory_space=pltpu.HBM)
    return pl.pallas_call(
        kernel,
        out_shape=[jax.ShapeDtypeStruct(s, d) for s, d in outputs]
        + [pltpu.HBM(s, d) for s, d in to_hbm],
        in_specs=[near if x.ndim > 1 else pl.BlockSpec(memory_space=pltpu.SMEM) for x in inputs]
        + [far] * len(held),
        out_specs=[near] * len(outputs) + [far] * len(to_hbm),
        scratch_shapes=list(scratch),
        compiler_params=pltpu.CompilerParams(vmem_limit_bytes=limit * MIB),
    )(*inputs, *held)


def to_all(blocks):
    value = jnp.concatenate(blocks, 0)
    copies = jnp.broadcast_to(value[None], (SUB,) + value.shape)
    return lax.all_to_all(copies, "sub", 0, 0, tiled=True)


def neighbours(on, off):
    count = lax.axis_size("dom")
    pairs = [(i, i + 1) for i in range(1, count - 1, 2)]
    from_off = lax.ppermute(off, "dom", pairs + [(j, i) for i, j in pairs])
    from_on = lax.ppermute(on, "dom", [(i, i ^ 1) for i in range(count)])
    even = lax.axis_index("dom") % 2 == 0
    return jnp.where(even, from_off, from_on), jnp.where(even, from_on, from_off)


def later(own, on, off):
    from_below, from_above = neighbours(on, off)
    return to_all([own[:LATER_UP], from_below[: FD + 1], from_above[: FD + 1]])


def on_device(
    interior_inverse, coupling, trace_block, interior_load, trace_load, face_shift, element_faces, block_padding,
):
    slab, rows8 = ((NF, LANES), F32), ((8, LANES), F32)
    places = ((8, LANES), jnp.int32)
    sent = [((64, LANES), I16), ((16, LANES), I16), ((16, LANES), I16)]
    stage = pltpu.VMEM((64, LANES), F32)
    decoded = pltpu.VMEM((SUB, LATER_ROWS, LANES), F32)
    decoded_first = pltpu.VMEM((SUB, FIRST_ROWS, LANES), F32)
    matrices = [interior_inverse, coupling, trace_block]

    inner = ((NI, LANES), F32)

    living, own, on, off, solved = call(
        first_kernel,
        [rows8, ((112, LANES), I16), ((32, LANES), I16), ((32, LANES), I16)],
        [block_padding],
        from_hbm=[interior_inverse, coupling, interior_load, trace_load, face_shift, element_faces],
        to_hbm=[inner],
        scratch=[
            pltpu.VMEM((NI, LANES), F32), pltpu.VMEM((NI, NI, LANES), BF16), pltpu.VMEM((NI, NF, LANES), BF16),
            pltpu.VMEM((NI, LANES), BF16), pltpu.VMEM((FD, 2 * RIM), F32), pltpu.VMEM((FD, 2 * RIM), F32),
            pltpu.VMEM((4, LANES), jnp.int32), pltpu.VMEM((112, LANES), F32),
            pltpu.SemaphoreType.DMA((PARTS + 6,)),
        ],
        limit=10,
    )
    *matrices, own = lax.optimization_barrier((*matrices, own))
    from_below, from_above = neighbours(on, off)
    first = to_all([own[:UP], from_below[: DOWN - UP], from_above[: FIRST_ROWS - DOWN]])
    chunk, lane, valid, weight, shifts, view0, terms, kept, scale, own, on, off = call(
        second_kernel,
        [places, places, rows8, rows8, slab, slab, slab, inner, rows8, *sent],
        [*matrices, element_faces, living, first],
        scratch=[pltpu.VMEM((NF, LANES), F32), stage, decoded_first],
    )
    second = later(own, on, off)
    view1, terms1, kept, scale, own, on, off = call(
        third_kernel,
        [slab, slab, ((2, NI, LANES), F32), rows8, *sent],
        [*matrices, element_faces, living, second, chunk, lane, valid, shifts, view0, terms, scale, kept],
        scratch=[stage, decoded],
    )
    third = later(own, on, off)
    partitions = lax.axis_size("dom")
    sums, for_mate, kept = call(
        fourth_kernel,
        [((1, LANES), F32), ((1, LANES), F32)],
        [*matrices, living, third, chunk, lane, valid, weight, shifts, view0, view1, terms1, scale, kept],
        to_hbm=[((3, NI, LANES), F32)],
        scratch=[
            pltpu.VMEM((NI, LANES), F32), decoded, pltpu.SemaphoreType.DMA((2,)),
        ],
    )
    sums = sums + lax.ppermute(for_mate, "dom", [(i, i ^ 1) for i in range(partitions)])
    members = [[d * SUB + s for d in range(core, partitions, 2) for s in range(SUB)] for core in range(2)]
    all_sums = lax.all_to_all(
        jnp.broadcast_to(sums, (len(members[0]), LANES)), ("dom", "sub"), 0, 0, tiled=True,
        axis_index_groups=members,
    )
    owned, kept = call(
        owner_kernel,
        [((3, FD, 2 * RIM), F32), ((4, NI, LANES), F32)],
        [first, second, third],
        from_hbm=[trace_load, face_shift, solved, kept],
        scratch=[
            pltpu.VMEM((144, 32 * LANES), BF16), pltpu.VMEM((2 * RIM, 32 * LANES), BF16),
            decoded_first, decoded, decoded,
            pltpu.VMEM((FD, 2 * RIM), F32), pltpu.VMEM((FD, 2 * RIM), F32), pltpu.SemaphoreType.DMA((4,)),
        ],
        limit=14,
    )
    traces, interior = call(
        last_kernel,
        [((FD, 2 * RIM), F32), ((NI, LANES), F32)],
        [living, all_sums, kept, owned],
    )
    return traces, interior


def solution(mesh):
    last = ("dom", "sub")
    placed = (
        P(None, None, last), P(None, None, last), P(None, None, last),
        P(None, last), P(None, last), P(None, last), P(None, last), P(last),
    )
    return jax.shard_map(
        on_device,
        mesh=mesh,
        in_specs=placed,
        out_specs=(P(None, last), P(None, last)),
        check_vma=False,
    )
```

```python
import functools

import jax
import jax.numpy as jnp
from jax import lax
from jax.experimental import pallas as pl
from jax.experimental.pallas import tpu as pltpu
from jax.sharding import PartitionSpec as P

NI = 80
FD = 12
NF = 48
LANES = 128
RIM = 128
SUB = 8
FACES_PART = 2048
F32 = jnp.float32
BF16 = jnp.bfloat16
MIB = 1024 * 1024
PARTS = 5

I16 = jnp.int16

BIAS = 16384.0
SCALE_LANE = 64
FACES, NAMES, SCALES, UP, UP_SHIFT, DOWN, FIRST_ROWS = 48, 96, 100, 105, 118, 131, 144
LATER_UP, LATER_DOWN, LATER_ROWS = 54, 67, 80


def row_iota(rows):
    return lax.broadcasted_iota(jnp.int32, (rows, LANES), 0)


def lane_iota(rows):
    return lax.broadcasted_iota(jnp.int32, (rows, LANES), 1)


def eight_sums(parts):
    rows = row_iota(8)
    low = rows < 4
    parts = [
        jnp.where(low, parts[i], parts[i + 4])
        + pltpu.roll(jnp.where(low, parts[i + 4], parts[i]), 4, 0)
        for i in range(4)
    ]
    for step in (2, 1):
        low = (rows & step) == 0
        parts = [
            jnp.where(
                low,
                parts[i] + pltpu.roll(parts[i], 8 - step, 0),
                parts[i + step] + pltpu.roll(parts[i + step], step, 0),
            )
            for i in range(step)
        ]
    return parts[0]


def matrix_times(matrix_ref, vector):
    rows, depth, _ = matrix_ref.shape
    blocks = []
    for first in range(0, rows, 8):
        parts = [
            (matrix_ref[first + i].astype(F32) * vector)
            .reshape(depth // 8, 8, LANES)
            .sum(0)
            for i in range(8)
        ]
        blocks.append(eight_sums(parts))
    return jnp.concatenate(blocks, 0)


def transposed_times(matrix_ref, vector):
    depth = matrix_ref.shape[0]
    totals = [None] * 4
    for i in range(depth):
        term = matrix_ref[i].astype(F32) * vector[i : i + 1]
        totals[i % 4] = term if totals[i % 4] is None else totals[i % 4] + term
    return (totals[0] + totals[1]) + (totals[2] + totals[3])


def coded(value):
    top = jnp.abs(value).max(0, keepdims=True).max(1, keepdims=True)
    exponent = jnp.floor(jnp.log2(jnp.maximum(top, 2.0**-100))) + 1.0
    whole = jnp.floor(value * jnp.exp2(15.0 - exponent) + 0.5)
    return jnp.clip(whole, -32767.0, 32767.0), exponent


def spread_row(exponent):
    return jnp.broadcast_to(exponent + BIAS, (1, LANES))


def as_sent(value):
    return value.astype(jnp.int32).astype(I16)


def with_exponent(value):
    whole, exponent = coded(value)
    return [whole, spread_row(exponent)]


def put_lists(on_ref, off_ref, up, down, dom):
    even = dom % 2 == 0
    rest = [jnp.zeros((on_ref.shape[0] - sum(len(x) for x in up), LANES), F32)]
    up, down = jnp.concatenate(up + rest, 0), jnp.concatenate(down + rest, 0)
    on_ref[...] = as_sent(jnp.where(even, up, down))
    off_ref[...] = as_sent(jnp.where(even, down, up))


def decode(sent_ref, terms_ref, sections, scale_rows, least=None):
    rows = sent_ref.shape[1]
    row = row_iota(rows)
    for s in range(SUB):
        terms_ref[s] = sent_ref[s].astype(jnp.int32).astype(F32)
    base = least
    for s in range(SUB):
        for place in scale_rows:
            exponent = terms_ref[s, place : place + 1, :] - BIAS
            base = exponent if base is None else jnp.maximum(base, exponent)
    for s in range(SUB):
        factors = jnp.ones((1, LANES), F32)
        for end, exponent, scaled in reversed(sections):
            if exponent is None:
                factor = jnp.ones((1, LANES), F32)
            else:
                power = terms_ref[s, exponent : exponent + 1, :] - (BIAS + 15.0)
                factor = jnp.exp2(power - base if scaled else power)
            factors = jnp.where(row < end, factor, factors)
        terms_ref[s] = terms_ref[s] * factors
    return base


def decode_first(sent_ref, terms_ref):
    return decode(
        sent_ref,
        terms_ref,
        [
            (FACES, SCALES, True), (FACES + FD, SCALES + 1, True), (FACES + 2 * FD, SCALES + 2, False),
            (FACES + 3 * FD, SCALES + 1, True), (NAMES, SCALES + 2, False), (UP, None, False),
            (UP + FD, UP + FD, True), (UP_SHIFT, None, False), (UP_SHIFT + FD, UP_SHIFT + FD, False),
            (DOWN, None, False), (FIRST_ROWS, DOWN + FD, True),
        ],
        (SCALES, SCALES + 1, UP + FD, DOWN + FD),
    )


def decode_later(sent_ref, terms_ref, before):
    return decode(
        sent_ref,
        terms_ref,
        [
            (NF, NF, True), (LATER_UP, None, False), (LATER_UP + FD, LATER_UP + FD, True),
            (LATER_DOWN, None, False), (LATER_ROWS, LATER_DOWN + FD, True),
        ],
        (NF, LATER_UP + FD, LATER_DOWN + FD),
        before + 3.0,
    )


def ids():
    return lax.axis_index("dom"), lax.axis_index("sub")


def element_operator(inverse_ref, coupling_ref, trace_ref, view, living_ref, keep):
    inner = matrix_times(inverse_ref, matrix_times(coupling_ref, view))
    keep(inner)
    terms = transposed_times(coupling_ref, inner) + matrix_times(trace_ref, view)
    return jnp.where(six_times(living_ref[...]) > 0.0, terms, 0.0)


def split3(value):
    high = value.astype(BF16)
    rest = value - high.astype(F32)
    middle = rest.astype(BF16)
    low = (rest - middle.astype(F32)).astype(BF16)
    return high, middle, low


def whole_pick(values, chosen):
    high = jnp.floor(values * (1.0 / 256.0))
    stacked = jnp.concatenate([high, values - 256.0 * high], 0).astype(BF16)
    sums = jnp.dot(stacked, chosen, preferred_element_type=F32)
    rows = values.shape[0]
    return 256.0 * sums[:rows] + sums[rows:]


def as_columns(rows):
    rest = jnp.zeros((LANES - len(rows), LANES), F32)
    return jnp.concatenate([rows, rest], 0).T.astype(jnp.int32)


def face_major(terms_ref):
    slots = []
    for j in range(4):
        part = terms_ref[pl.ds(j, FD, stride=4), :]
        slots.append(jnp.concatenate([part, jnp.zeros((4, LANES), F32)], 0))
    return jnp.concatenate(slots, 1)


def rim_lists(terms_ref, names_ref):
    turned = as_columns(names_ref[...].astype(F32))
    wanted = lane_iota(LANES)
    chosen = []
    for j in range(4):
        name = jnp.broadcast_to(turned[:, j : j + 1], (LANES, LANES))
        hits = [name == wanted, name == wanted + FACES_PART]
        chosen.append(jnp.concatenate([jnp.where(hit, 1.0, 0.0).astype(BF16) for hit in hits], 1))
    lists = whole_pick(face_major(terms_ref), jnp.concatenate(chosen, 0))
    return lists[:FD, :RIM], lists[:FD, RIM:]


def first_kernel(
    padding_ref, inverse_hbm, coupling_hbm, interior_load_hbm, trace_load_hbm, shift_hbm, names_hbm,
    living_ref, own_ref, on_ref, off_ref, solved_hbm,
    solved_ref, inverse_ref, coupling_ref, interior_load_ref, trace_load_ref, shift_ref, names_ref, stage_ref, sems,
):
    rows = NI // PARTS
    copies = [pltpu.make_async_copy(interior_load_hbm, interior_load_ref, sems.at[0])]
    for part in range(PARTS):
        block = pl.ds(part * rows, rows)
        copies.append(
            pltpu.make_async_copy(inverse_hbm.at[block], inverse_ref.at[block], sems.at[1 + part])
        )
    rest = [
        (coupling_hbm, coupling_ref), (names_hbm, names_ref),
        (trace_load_hbm, trace_load_ref), (shift_hbm, shift_ref),
    ]
    for place, (source, target) in enumerate(rest):
        copies.append(pltpu.make_async_copy(source, target, sems.at[1 + PARTS + place]))
    for copy in [copies[0], copies[1 + PARTS], *copies[2 + PARTS :], *copies[1 : 1 + PARTS]]:
        copy.start()
    dom, sub = ids()
    for copy in copies[2 + PARTS :]:
        copy.wait()
    living = lane_iota(1) < LANES - padding_ref[0]
    living_ref[...] = jnp.broadcast_to(jnp.where(living, 1.0, 0.0), (8, LANES))
    stage_ref[NAMES:, :] = jnp.zeros((stage_ref.shape[0] - NAMES, LANES), F32)
    loads, load_exponent = coded(trace_load_ref[...])
    shifts, shift_exponent = coded(shift_ref[...])
    for half in range(2):
        columns = slice(half * RIM, half * RIM + RIM)
        first = FACES + 2 * FD * half
        stage_ref[first : first + FD, :] = loads[:, columns]
        stage_ref[first + FD : first + 2 * FD, :] = shifts[:, columns]
    stage_ref[NAMES : NAMES + 4, :] = names_ref[...].astype(F32)
    stage_ref[SCALES + 1 : SCALES + 2, :] = spread_row(load_exponent)
    stage_ref[SCALES + 2 : SCALES + 3, :] = spread_row(shift_exponent)
    copies[0].wait()
    load = interior_load_ref[...].astype(F32)
    solved = []
    for part in range(PARTS):
        copies[1 + part].wait()
        solved.append(matrix_times(inverse_ref.at[pl.ds(part * rows, rows)], load))
    solved = jnp.concatenate(solved, 0)
    solved_ref[...] = solved
    keep = pltpu.make_async_copy(solved_ref, solved_hbm, sems.at[PARTS + 5])
    keep.start()
    copies[1 + PARTS].wait()
    whole, exponent = coded(jnp.where(living, transposed_times(coupling_ref, solved), 0.0))
    stage_ref[:NF, :] = whole
    stage_ref[SCALES : SCALES + 1, :] = spread_row(exponent)
    low, high = rim_lists(stage_ref, names_ref)
    owner = sub == SUB - 1
    up = with_exponent(
        high * jnp.exp2(exponent - 15.0) + jnp.where(owner, trace_load_ref[:, RIM:], 0.0)
    )
    up += [jnp.where(owner, shifts[:, RIM:], 0.0), spread_row(shift_exponent)]
    down = [low, spread_row(exponent), jnp.zeros((FD + 1, LANES), F32)]
    put_lists(on_ref, off_ref, up, down, dom)
    own_ref[...] = as_sent(stage_ref[...])
    keep.wait()


def spread_rows(values, block):
    a = jnp.broadcast_to(values[2 * block : 2 * block + 1], (8, LANES))
    b = jnp.broadcast_to(values[2 * block + 1 : 2 * block + 2], (8, LANES))
    return jnp.where(row_iota(8) < 4, a, b)


def turn(values, steps):
    if steps == 0:
        return values
    rows = row_iota(8) & 3
    return jnp.where(
        rows < 4 - steps, pltpu.roll(values, 8 - steps, 0), pltpu.roll(values, 4 - steps, 0)
    )


def take_lanes(values, lanes):
    return jnp.take_along_axis(values, lanes, axis=1, mode="promise_in_bounds")


def partner_terms(gathered_ref, chunk, lane, low_list, high_list):
    rows = row_iota(8) & 3
    found = [jnp.zeros((8, LANES), F32) for _ in range(6)]
    for t in range(4):
        chunk_t = turn(chunk, (4 - t) % 4)
        lane_t = turn(lane, (4 - t) % 4)
        part = [jnp.zeros((8, LANES), F32) for _ in range(6)]
        for s in range(SUB):
            here = chunk_t == 4 * s + rows
            for g in range(6):
                taken = take_lanes(gathered_ref[s, 8 * g : 8 * g + 8, :], lane_t)
                part[g] = jnp.where(here, taken, part[g])
        for g in range(6):
            found[g] = found[g] + turn(part[g], t)
    on_low = chunk == 4 * SUB
    on_high = chunk == 4 * SUB + 1
    for g in range(6):
        found[g] = jnp.where(on_low, take_lanes(spread_rows(low_list, g), lane), found[g])
        found[g] = jnp.where(on_high, take_lanes(spread_rows(high_list, g), lane), found[g])
    return jnp.concatenate(found, 0)


def twice(slots):
    return jnp.concatenate([slots, slots], 0)


def six_times(rows8):
    return jnp.concatenate([rows8] * 6, 0)


def summed(gathered_ref, first, last):
    total = gathered_ref[0, first:last, :]
    for s in range(1, SUB):
        total = total + gathered_ref[s, first:last, :]
    return total


def partner_places(names_ref, gathered_ref, sub):
    weights, columns = [], []
    high_rows = row_iota(24)
    low_rows = row_iota(LANES)
    for s in range(SUB):
        for j in range(4):
            names = gathered_ref[s, NAMES + j : NAMES + j + 1, :].astype(jnp.int32)
            row_hit = (names >> 7) == high_rows
            weights.append(
                jnp.concatenate(
                    [
                        jnp.where(row_hit, F32(4 * s + j), 0.0),
                        jnp.where(row_hit, lane_iota(24).astype(F32), 0.0),
                    ],
                    0,
                ).astype(BF16)
            )
            columns.append(jnp.where((names & 127) == low_rows, 1.0, 0.0).astype(BF16))
    table = lax.dot_general(
        jnp.concatenate(weights, 1),
        jnp.concatenate(columns, 1),
        (((1,), (1,)), ((), ())),
        preferred_element_type=F32,
    )
    chunks, lanes = [], []
    for j in range(4):
        name = names_ref[j : j + 1, :]
        low = jnp.broadcast_to(name & 127, (24, LANES))
        hit = high_rows == (name >> 7)
        chunk_sum = jnp.where(hit, take_lanes(table[:24], low), 0.0).sum(0, keepdims=True)
        lane_sum = jnp.where(hit, take_lanes(table[24:], low), 0.0).sum(0, keepdims=True)
        chunk = chunk_sum.astype(jnp.int32) - (4 * sub + j)
        lane = lane_sum.astype(jnp.int32) - lane_iota(1)
        below, above = name < RIM, name >= FACES_PART
        chunk = jnp.where(below, 4 * SUB, jnp.where(above, 4 * SUB + 1, chunk))
        lane = jnp.where(below | above, name & 127, lane)
        chunks.append(chunk)
        lanes.append(lane)
    return jnp.concatenate(chunks, 0), jnp.concatenate(lanes, 0) & 127


def face_values(names_ref, gathered_ref, up_list, loads_ref, shifts_ref):
    for j in range(4):
        name = names_ref[j : j + 1, :]
        high = jnp.broadcast_to(name >> 7, (24, LANES))
        low = jnp.broadcast_to(name & 127, (24, LANES))
        got = jnp.where(high == 0, take_lanes(up_list, low), 0.0)
        for s in range(SUB):
            for half in range(2):
                first = FACES + 2 * FD * half
                source = gathered_ref[s, first : first + 2 * FD, :]
                got = jnp.where(high == 2 * s + half + 1, take_lanes(source, low), got)
        loads_ref[pl.ds(j, FD, stride=4), :] = got[:FD]
        shifts_ref[pl.ds(j, FD, stride=4), :] = got[FD:]


def put_terms(terms, base, names_ref, own_ref, on_ref, off_ref, stage_ref, dom):
    whole, exponent = coded(terms)
    exponent = exponent + base
    stage_ref[:NF, :] = whole
    stage_ref[NF:, :] = jnp.broadcast_to(exponent + BIAS, (stage_ref.shape[0] - NF, LANES))
    own_ref[...] = as_sent(stage_ref[...])
    low, high = rim_lists(stage_ref, names_ref)
    put_lists(on_ref, off_ref, [high, spread_row(exponent)], [low, spread_row(exponent)], dom)


def second_kernel(
    inverse_ref, coupling_ref, trace_ref, names_ref, living_ref, sent_ref,
    chunk_ref, lane_ref, valid_ref, weight_ref, shifts_ref, view_ref, terms_ref, inner_ref, scale_ref, own_ref, on_ref, off_ref,
    loads_ref, stage_ref, gathered_ref,
):
    dom, sub = ids()
    count = lax.axis_size("dom")
    base = decode_first(sent_ref, gathered_ref)
    scale_ref[...] = jnp.broadcast_to(base, (8, LANES))
    chunk, lane = partner_places(names_ref, gathered_ref, sub)
    chunk, lane = twice(chunk), twice(lane)
    names = twice(names_ref[...])
    valid = jnp.where((names < RIM) & (dom == 0), 0.0, 1.0)
    weight = jnp.where((names >= FACES_PART) & (dom == count - 1), 1.0, 0.5)
    chunk_ref[...] = chunk
    lane_ref[...] = lane
    valid_ref[...] = valid
    weight_ref[...] = weight
    up_list = jnp.concatenate(
        [summed(gathered_ref, UP, UP + FD), summed(gathered_ref, UP_SHIFT, UP_SHIFT + FD)], 0
    )
    down_list = summed(gathered_ref, DOWN, DOWN + FD)
    face_values(names_ref, gathered_ref, up_list, loads_ref, shifts_ref)
    own_load = jnp.where(six_times(names) < RIM, 0.0, loads_ref[...])
    partner = partner_terms(gathered_ref, chunk, lane, up_list[:FD], down_list)
    view = jnp.where(six_times(valid) > 0.0, own_load + (gathered_ref[sub, :NF, :] + partner), 0.0)
    view_ref[...] = view
    def keep(inner):
        inner_ref[...] = inner

    terms = element_operator(inverse_ref, coupling_ref, trace_ref, view, living_ref, keep)
    terms_ref[...] = terms
    put_terms(terms, base, names_ref, own_ref, on_ref, off_ref, stage_ref, dom)


def next_view(factor, gathered_ref, chunk_ref, lane_ref, valid_ref, shifts_ref, view_ref, terms_ref):
    low_list = summed(gathered_ref, LATER_UP, LATER_UP + FD)
    high_list = summed(gathered_ref, LATER_DOWN, LATER_DOWN + FD)
    partner = partner_terms(gathered_ref, chunk_ref[...], lane_ref[...], low_list, high_list)
    image = factor * (terms_ref[...] + shifts_ref[...] * view_ref[...]) + partner
    return jnp.where(six_times(valid_ref[...]) > 0.0, image, 0.0)


def third_kernel(
    inverse_ref, coupling_ref, trace_ref, names_ref, living_ref, sent_ref,
    chunk_ref, lane_ref, valid_ref, shifts_ref, view_ref, terms_ref, scale_ref, before_ref,
    new_view_ref, new_terms_ref, inner_ref, new_scale_ref, own_ref, on_ref, off_ref,
    stage_ref, gathered_ref,
):
    dom, _ = ids()
    scale = scale_ref[:1, :]
    base = decode_later(sent_ref, gathered_ref, scale)
    new_scale_ref[...] = jnp.where(row_iota(8) == 0, scale, base)
    factor = jnp.exp2(scale - base)
    view = next_view(factor, gathered_ref, chunk_ref, lane_ref, valid_ref, shifts_ref, view_ref, terms_ref)
    new_view_ref[...] = view
    inner_ref[0] = before_ref[...]

    def keep(inner):
        inner_ref[1] = inner

    terms = element_operator(inverse_ref, coupling_ref, trace_ref, view, living_ref, keep)
    new_terms_ref[...] = terms
    put_terms(terms, base, names_ref, own_ref, on_ref, off_ref, stage_ref, dom)


def fourth_kernel(
    inverse_ref, coupling_ref, trace_ref, living_ref, sent_ref,
    chunk_ref, lane_ref, valid_ref, weight_ref, shifts_ref, first_view_ref, view_ref, terms_ref, scale_ref, before_ref,
    inner_hbm, sums_hbm,
    inner_ref, sums_ref, gathered_ref, sems,
):
    copies = [
        pltpu.make_async_copy(before_ref, inner_hbm.at[pl.ds(0, 2)], sems.at[0]),
        pltpu.make_async_copy(inner_ref, inner_hbm.at[2], sems.at[1]),
    ]
    copies[0].start()

    def keep(inner):
        inner_ref[...] = inner
        copies[1].start()

    scales = [scale_ref[:1, :], scale_ref[1:2, :]]
    scales.append(decode_later(sent_ref, gathered_ref, scales[1]))
    factor = jnp.exp2(scales[1] - scales[2])
    first, second = first_view_ref[...], view_ref[...]
    third = next_view(factor, gathered_ref, chunk_ref, lane_ref, valid_ref, shifts_ref, view_ref, terms_ref)
    last = element_operator(inverse_ref, coupling_ref, trace_ref, third, living_ref, keep)
    weight = six_times(weight_ref[...])
    last = last + weight * (shifts_ref[...] * third)
    views = (first, second, third)
    weighted = [weight * view for view in views]
    products = [weighted[i] * views[j] for i in range(3) for j in range(i, 3)]
    products += [view * last for view in views]
    powers = [scales[i] + scales[j] for i in range(3) for j in range(i, 3)]
    powers += [scale + scales[2] for scale in scales]
    lane = lane_iota(1)
    sums = jnp.zeros((1, LANES), F32)
    for place, product in enumerate(products):
        sums = sums + jnp.where(lane == SCALE_LANE + place, powers[place], 0.0)
        total = product.reshape(6, 8, LANES).sum(0).sum(0, keepdims=True).sum(1, keepdims=True)
        sums = sums + jnp.where(lane == place, total, 0.0)
    sums_ref[...] = jnp.broadcast_to(sums, sums_ref.shape)
    send = pltpu.make_async_copy(sums_ref, sums_hbm, sems.at[2])
    send.start()
    for copy in copies:
        copy.wait()
    send.wait()


def owner_kernel(
    first_sent_ref, second_sent_ref, third_sent_ref, trace_load_hbm, shift_hbm, *rest,
):
    solved_hbm, inner_hbm = rest[:2]
    owned_ref, kept_ref, terms_ref, chosen_ref, first_ref, second_ref, third_ref = rest[2:9]
    trace_load_ref, shift_ref, sems = rest[9:]
    copies = [
        pltpu.make_async_copy(trace_load_hbm, trace_load_ref, sems.at[0]),
        pltpu.make_async_copy(shift_hbm, shift_ref, sems.at[1]),
        pltpu.make_async_copy(solved_hbm, kept_ref.at[0], sems.at[2]),
        pltpu.make_async_copy(inner_hbm, kept_ref.at[pl.ds(1, 3)], sems.at[3]),
    ]
    for copy in copies:
        copy.start()
    scales = [decode_first(first_sent_ref, first_ref)]
    scales.append(decode_later(second_sent_ref, second_ref, scales[0]))
    scales.append(decode_later(third_sent_ref, third_ref, scales[1]))
    _, sub = ids()
    wanted = lax.broadcasted_iota(jnp.int32, (2 * RIM, LANES), 0) + (RIM + 2 * RIM * sub)
    sources = (first_ref, second_ref, third_ref)
    for s in range(SUB):
        for j in range(4):
            columns = slice((4 * s + j) * LANES, (4 * s + j + 1) * LANES)
            names = first_ref[s, NAMES + j : NAMES + j + 1, :].astype(jnp.int32)
            chosen_ref[:, columns] = jnp.where(wanted == names, 1.0, 0.0).astype(BF16)
            for v, source in enumerate(sources):
                part = source[s, pl.ds(j, FD, stride=4), :]
                part = jnp.concatenate([part, jnp.zeros((4, LANES), F32)], 0)
                for piece, value in enumerate(split3(part)):
                    first = 16 * (3 * v + piece)
                    terms_ref[first : first + 16, columns] = value
    sums = lax.dot_general(
        terms_ref[...], chosen_ref[...], (((1,), (1,)), ((), ())), preferred_element_type=F32
    )
    for copy in copies:
        copy.wait()
    last = sub == SUB - 1
    downs = (
        summed(first_ref, DOWN, DOWN + FD),
        summed(second_ref, LATER_DOWN, LATER_DOWN + FD),
        summed(third_ref, LATER_DOWN, LATER_DOWN + FD),
    )
    current = None
    for v in range(3):
        rows = [sums[48 * v + 16 * piece : 48 * v + 16 * piece + FD] for piece in range(3)]
        total = rows[0] + rows[1] + rows[2]
        down = jnp.concatenate(
            [jnp.zeros((FD, RIM), F32), jnp.where(last, downs[v], 0.0)], 1
        )
        total = total + down
        if v == 0:
            current = total + jnp.exp2(-scales[0][:, :1]) * trace_load_ref[...]
        else:
            factor = jnp.exp2(scales[v - 1] - scales[v])[:, :1]
            current = total + factor * (shift_ref[...] * current)
        owned_ref[v] = current


def coefficients(sums, powers, own_powers):
    lane = lane_iota(1)

    def entry(row, place):
        return jnp.where(lane == place, row, 0.0).sum(1, keepdims=True)

    pairs = [(i, j) for i in range(3) for j in range(i, 3)]
    pairs += [(i, 3) for i in range(3)]
    places = [pairs.index((i, i)) for i in range(3)]
    scales = [0.5 * entry(powers, place) for place in places]
    own_scales = [0.5 * entry(own_powers, place) for place in places]
    table = {}
    for place, (i, j) in enumerate(pairs):
        power = entry(powers, place) - scales[i] - scales[min(j, 2)]
        table[i, j] = table[j, i] = entry(sums, place) * jnp.exp2(power)
    steps = [jnp.exp2(scales[1] - scales[0]), jnp.exp2(scales[2] - scales[1]), 1.0]

    def form(left, right):
        total = None
        for i, a in enumerate(left):
            for j, b in enumerate(right):
                if a is None or b is None:
                    continue
                term = a * b * table[i, j]
                total = term if total is None else total + term
        return total

    def combine(left, factor, right):
        merged = []
        for i in range(max(len(left), len(right))):
            a = left[i] if i < len(left) else None
            b = right[i] if i < len(right) else None
            if b is None:
                merged.append(a)
            else:
                merged.append(factor * b if a is None else a + factor * b)
        return merged

    one = jnp.ones((1, 1), F32)
    residual, direction, result = [one], [one], []
    norm = table[0, 0]
    for iteration in range(3):
        image = [None] + [a * b for a, b in zip(direction, steps, strict=False)]
        step = norm / form(direction, image)
        result = combine(result, step, direction)
        if iteration < 2:
            residual = combine(residual, -step, image)
            new_norm = form(residual, residual)
            direction = combine(residual, new_norm / norm, direction)
            norm = new_norm
    return [
        part * jnp.exp2(scales[0] - scale + own)
        for part, scale, own in zip(result, scales, own_scales, strict=True)
    ]


def last_kernel(
    living_ref, all_sums_ref, inner_ref, owned_ref,
    traces_ref, interior_ref,
):
    dom, sub = ids()
    sums = all_sums_ref[...]
    powers = pltpu.roll(sums, LANES - SCALE_LANE, 1)
    own = pltpu.roll(all_sums_ref[pl.ds(dom * SUB + sub, 1), :], LANES - SCALE_LANE, 1)
    used = lane_iota(1) < SCALE_LANE
    powers, own = jnp.where(used, powers, 0.0), jnp.where(used, own, 0.0)
    top = powers.reshape(-1, 8, LANES).max(0).max(0, keepdims=True)
    sums = (sums * jnp.exp2(powers - top)).reshape(-1, 8, LANES).sum(0).sum(0, keepdims=True)
    a, b, c = coefficients(sums, top, own)
    traces_ref[...] = a * owned_ref[0] + b * owned_ref[1] + c * owned_ref[2]
    lifted = a * inner_ref[1] + b * inner_ref[2] + c * inner_ref[3]
    living = jnp.broadcast_to(living_ref[:1, :], (NI, LANES)) > 0.0
    interior_ref[...] = jnp.where(living, inner_ref[0] - lifted, 0.0)


def call(kernel, outputs, inputs, scratch=(), limit=6, from_hbm=(), to_hbm=()):
    held = [pltpu.with_memory_space_constraint(x, pltpu.HBM) for x in from_hbm]
    near, far = pl.BlockSpec(memory_space=pltpu.VMEM), pl.BlockSpec(memory_space=pltpu.HBM)
    return pl.pallas_call(
        kernel,
        out_shape=[jax.ShapeDtypeStruct(s, d) for s, d in outputs]
        + [pltpu.HBM(s, d) for s, d in to_hbm],
        in_specs=[near if x.ndim > 1 else pl.BlockSpec(memory_space=pltpu.SMEM) for x in inputs]
        + [far] * len(held),
        out_specs=[near] * len(outputs) + [far] * len(to_hbm),
        scratch_shapes=list(scratch),
        compiler_params=pltpu.CompilerParams(vmem_limit_bytes=limit * MIB),
    )(*inputs, *held)


def to_all(blocks):
    value = jnp.concatenate(blocks, 0)
    copies = jnp.broadcast_to(value[None], (SUB,) + value.shape)
    return lax.all_to_all(copies, "sub", 0, 0, tiled=True)


def neighbours(on, off):
    count = lax.axis_size("dom")
    pairs = [(i, i + 1) for i in range(1, count - 1, 2)]
    from_off = lax.ppermute(off, "dom", pairs + [(j, i) for i, j in pairs])
    from_on = lax.ppermute(on, "dom", [(i, i ^ 1) for i in range(count)])
    even = lax.axis_index("dom") % 2 == 0
    return jnp.where(even, from_off, from_on), jnp.where(even, from_on, from_off)


def later(own, on, off):
    from_below, from_above = neighbours(on, off)
    return to_all([own[:LATER_UP], from_below[: FD + 1], from_above[: FD + 1]])


def on_device(
    interior_inverse, coupling, trace_block, interior_load, trace_load, face_shift, element_faces, block_padding,
):
    slab, rows8 = ((NF, LANES), F32), ((8, LANES), F32)
    places = ((8, LANES), jnp.int32)
    sent = [((64, LANES), I16), ((16, LANES), I16), ((16, LANES), I16)]
    stage = pltpu.VMEM((64, LANES), F32)
    decoded = pltpu.VMEM((SUB, LATER_ROWS, LANES), F32)
    decoded_first = pltpu.VMEM((SUB, FIRST_ROWS, LANES), F32)
    matrices = [interior_inverse, coupling, trace_block]

    inner = ((NI, LANES), F32)

    living, own, on, off, solved = call(
        first_kernel,
        [rows8, ((112, LANES), I16), ((32, LANES), I16), ((32, LANES), I16)],
        [block_padding],
        from_hbm=[interior_inverse, coupling, interior_load, trace_load, face_shift, element_faces],
        to_hbm=[inner],
        scratch=[
            pltpu.VMEM((NI, LANES), F32), pltpu.VMEM((NI, NI, LANES), BF16), pltpu.VMEM((NI, NF, LANES), BF16),
            pltpu.VMEM((NI, LANES), BF16), pltpu.VMEM((FD, 2 * RIM), F32), pltpu.VMEM((FD, 2 * RIM), F32),
            pltpu.VMEM((4, LANES), jnp.int32), pltpu.VMEM((112, LANES), F32),
            pltpu.SemaphoreType.DMA((PARTS + 6,)),
        ],
        limit=10,
    )
    *matrices, own = lax.optimization_barrier((*matrices, own))
    from_below, from_above = neighbours(on, off)
    first = to_all([own[:UP], from_below[: DOWN - UP], from_above[: FIRST_ROWS - DOWN]])
    chunk, lane, valid, weight, shifts, view0, terms, kept, scale, own, on, off = call(
        second_kernel,
        [places, places, rows8, rows8, slab, slab, slab, inner, rows8, *sent],
        [*matrices, element_faces, living, first],
        scratch=[pltpu.VMEM((NF, LANES), F32), stage, decoded_first],
    )
    second = later(own, on, off)
    view1, terms1, kept, scale, own, on, off = call(
        third_kernel,
        [slab, slab, ((2, NI, LANES), F32), rows8, *sent],
        [*matrices, element_faces, living, second, chunk, lane, valid, shifts, view0, terms, scale, kept],
        scratch=[stage, decoded],
    )
    third = later(own, on, off)
    everyone = lax.axis_size("dom") * SUB
    kept, sums = call(
        fourth_kernel,
        [],
        [*matrices, living, third, chunk, lane, valid, weight, shifts, view0, view1, terms1, scale, kept],
        to_hbm=[((3, NI, LANES), F32), ((everyone, LANES), F32)],
        scratch=[
            pltpu.VMEM((NI, LANES), F32), pltpu.VMEM((everyone, LANES), F32), decoded,
            pltpu.SemaphoreType.DMA((3,)),
        ],
    )
    all_sums = lax.all_to_all(sums, ("dom", "sub"), 0, 0, tiled=True)
    owned, kept = call(
        owner_kernel,
        [((3, FD, 2 * RIM), F32), ((4, NI, LANES), F32)],
        [first, second, third],
        from_hbm=[trace_load, face_shift, solved, kept],
        scratch=[
            pltpu.VMEM((144, 32 * LANES), BF16), pltpu.VMEM((2 * RIM, 32 * LANES), BF16),
            decoded_first, decoded, decoded,
            pltpu.VMEM((FD, 2 * RIM), F32), pltpu.VMEM((FD, 2 * RIM), F32), pltpu.SemaphoreType.DMA((4,)),
        ],
        limit=14,
    )
    traces, interior = call(
        last_kernel,
        [((FD, 2 * RIM), F32), ((NI, LANES), F32)],
        [living, all_sums, kept, owned],
    )
    return traces, interior


def solution(mesh):
    last = ("dom", "sub")
    placed = (
        P(None, None, last), P(None, None, last), P(None, None, last),
        P(None, last), P(None, last), P(None, last), P(None, last), P(last),
    )
    return jax.shard_map(
        on_device,
        mesh=mesh,
        in_specs=placed,
        out_specs=(P(None, last), P(None, last)),
        check_vma=False,
    )
```
